128 devices in a mesh: clip: 32 (over y, z, x_lo), seq: 4 (over x_hi, core).
Axes of the slice: x: 4 (x_hi: 2, x_lo: 2; x = x_hi * 2 + x_lo), y: 4, z: 4, core: 2. Of those that a mesh axis runs over, the one named last changes fastest.
Arguments:
- latents: bfloat16 [32, 4, 160, 1152], P('clip', 'seq'), may hold values from -6 to 6
- noise_sample: bfloat16 [32, 4, 160, 1152], P('clip', 'seq'), may hold values from -6 to 6
- timesteps: int32 [32], P('clip'), may hold values from 0 to 999
- text_states: bfloat16 [32, 120, 4096], P('clip'), may hold values from -6 to 6
- text_lengths: int32 [32], P('clip'), may hold values from 91 to 120, as said below
- cotangent: bfloat16 [32, 4, 160, 1152], P('clip', 'seq'), may hold values from -6 to 6
- time_input: bfloat16 [256, 1152], P(('clip', 'seq')), may hold values from -0.375 to 0.375
- time_output: bfloat16 [1152, 6912], P(('clip', 'seq')), may hold values from -0.1875 to 0.1875
- spatial_table: bfloat16 [6, 1152], P(None, ('clip', 'seq')), may hold values from -3 to 3
- spatial_projection: bfloat16 [1152, 3456], P(('clip', 'seq')), may hold values from -0.1875 to 0.1875
- spatial_output: bfloat16 [1152, 1152], P(('clip', 'seq')), may hold values from -0.625 to 0.625
- spatial_up: bfloat16 [1152, 4608], P(('clip', 'seq')), may hold values from -0.1875 to 0.1875
- spatial_down: bfloat16 [4608, 1152], P(('clip', 'seq')), may hold values from -0.09375 to 0.09375
- temporal_table: bfloat16 [6, 1152], P(None, ('clip', 'seq')), may hold values from -3 to 3
- temporal_projection: bfloat16 [1152, 3456], P(('clip', 'seq')), may hold values from -0.1875 to 0.1875
- temporal_output: bfloat16 [1152, 1152], P(('clip', 'seq')), may hold values from -0.25 to 0.25
- cross_query: bfloat16 [1152, 1152], P(('clip', 'seq')), may hold values from -0.1875 to 0.1875
- cross_text: bfloat16 [4096, 2304], P(('clip', 'seq')), may hold values from -0.09375 to 0.09375
- cross_output: bfloat16 [1152, 1152], P(('clip', 'seq')), may hold values from -0.5 to 0.5
- cross_gain: bfloat16 [1152], P(('clip', 'seq')), may hold values from 0.099609375 to 1.8984375
- temporal_up: bfloat16 [1152, 4608], P(('clip', 'seq')), may hold values from -0.1875 to 0.1875
- temporal_down: bfloat16 [4608, 1152], P(('clip', 'seq')), may hold values from -0.09375 to 0.09375
Outputs:
- activations: bfloat16 [32, 4, 160, 1152], P('clip', 'seq')
- latent_grad: float32 [32, 4, 160, 1152], P('clip', 'seq')
- grad_time_input: float32 [256, 1152], P(('clip', 'seq'))
- grad_time_output: float32 [1152, 6912], P(('clip', 'seq'))
- grad_spatial_table: float32 [6, 1152], P(None, ('clip', 'seq'))
- grad_spatial_projection: float32 [1152, 3456], P(('clip', 'seq'))
- grad_spatial_output: float32 [1152, 1152], P(('clip', 'seq'))
- grad_spatial_up: float32 [1152, 4608], P(('clip', 'seq'))
- grad_spatial_down: float32 [4608, 1152], P(('clip', 'seq'))
- grad_temporal_table: float32 [6, 1152], P(None, ('clip', 'seq'))
- grad_temporal_projection: float32 [1152, 3456], P(('clip', 'seq'))
- grad_temporal_output: float32 [1152, 1152], P(('clip', 'seq'))
- grad_cross_query: float32 [1152, 1152], P(('clip', 'seq'))
- grad_cross_text: float32 [4096, 2304], P(('clip', 'seq'))
- grad_cross_output: float32 [1152, 1152], P(('clip', 'seq'))
- grad_cross_gain: float32 [1152], P(('clip', 'seq'))
- grad_temporal_up: float32 [1152, 4608], P(('clip', 'seq'))
- grad_temporal_down: float32 [4608, 1152], P(('clip', 'seq'))
The draws below stay inside these ranges and needn't reach their ends.
Inputs may be any that keep to these rules, and one draw needn't show every extreme that they name: Each clip's caption uses its first text_lengths tokens; some clip uses all 120.
All inputs are finite; a program needn't handle non-finite values.
Results may differ from the reference program's by a relative error of at most 0.035.
Values may be sent and summed in bfloat16 or wider, within the bound.
No kernel may reach another device: no remote copies, remote signals or barrier semaphores. Data moves between devices by JAX's collectives and lax.ppermute only.
A program may use at most 640 MiB of HBM per device.

```python
import math
import jax
import jax.numpy as jnp
from jax import lax

HEADS = 16
HEAD_DIM = 72
FFN = 4608
TEXT_DIM = 4096
FREQ = 256
TEXT = 120
STEPS = 1000
PATCHES = 160
D = 1152
FRAMES = 4
CLIPS = 32


def draw_text_lengths(key, part):
    key = jax.random.fold_in(key, 7)
    draw_key, pick_key = jax.random.split(key)
    lengths = jax.random.randint(draw_key, (CLIPS,), 3 * TEXT // 4 + 1, TEXT + 1)
    chosen = jax.random.randint(pick_key, (), 0, CLIPS)
    return jnp.where(jnp.arange(CLIPS) == chosen, TEXT, lengths).astype(jnp.int32)


def set_ends(drawn, own_key, least, largest):
    index_at = [jax.random.randint(jax.random.fold_in(own_key, axis), (), 0, length) for axis, length in enumerate(drawn.shape)]
    main_axis = drawn.shape.index(max(drawn.shape))
    neighbour = index_at[:main_axis] + [(index_at[main_axis] + 1) % drawn.shape[main_axis]] + index_at[main_axis + 1:]
    return drawn.at[tuple(index_at)].set(least).at[tuple(neighbour)].set(largest)


def spiked(array, rng, source, target, parts, factor):
    def block_of(position):
        return (jnp.arange(array.shape[position]) // (array.shape[position] // parts)).reshape((-1,) + (1,) * (array.ndim - 1 - position))

    near = jax.random.permutation(rng, parts)[block_of(target)]
    other_side = (block_of(target) + parts // 2) % parts
    return jnp.where((block_of(source) == near) | (block_of(source) == other_side), factor * array, array)


def shard_levels(rng, dims, cuts, low, high):
    gain = 1.0
    for position, blocks in cuts:
        heights = jax.random.uniform(jax.random.fold_in(jax.random.fold_in(rng, 6), position), (blocks,), jnp.float32, low / len(cuts), high / len(cuts))
        gain = gain * jnp.repeat(jnp.exp(heights), dims[position] // blocks).reshape((-1,) + (1,) * (len(dims) - 1 - position))
    return gain


def bell_draw(stream_key, extent, scale, limit, cuts=(), held_as=jnp.bfloat16):
    drawn = jax.random.normal(stream_key, extent, jnp.float32) * scale
    if len(cuts) > 0:
        drawn = shard_levels(stream_key, extent, cuts, -0.22, 0.18) * drawn
    return jnp.clip(drawn, min=-limit, max=limit).astype(held_as)


def gaussian_with(own_key, extent, spread, limit, shards, heavy, kind=jnp.bfloat16):
    values = spread * jax.random.normal(own_key, extent, jnp.float32)
    if shards:
        values = values * shard_levels(own_key, extent, shards, -0.22, 0.18)
    return jnp.clip(spiked(values, jax.random.fold_in(own_key, 3), *heavy), -limit, limit).astype(kind)


def setup_inputs(seed: int = 0) -> dict:
    keys = jax.random.split(jax.random.key(seed), 23)
    return {
        "latents": bell_draw(keys[0], (CLIPS, FRAMES, PATCHES, D), 1.0, 6.0, ((0, 32), (1, 4))),
        "noise_sample": bell_draw(keys[1], (CLIPS, FRAMES, PATCHES, D), 1.0, 6.0, ((0, 32), (1, 4))),
        "timesteps": set_ends(jax.random.randint(keys[2], (CLIPS,), 0, STEPS), jax.random.fold_in(keys[2], 1), 0, STEPS - 1).astype(jnp.int32),
        "text_states": bell_draw(keys[3], (CLIPS, TEXT, TEXT_DIM), 1.0, 6.0, ((0, 32),)),
        "text_lengths": draw_text_lengths(jax.random.fold_in(keys[22], 71), 0),
        "cotangent": gaussian_with(keys[5], (CLIPS, FRAMES, PATCHES, D), 1.0, 6.0, ((0, 32), (1, 4)), (0, 3, 32, 2.75)),
        "time_input": bell_draw(keys[6], (FREQ, D), FREQ ** -0.5, 0.375, ((0, 128),)),
        "time_output": bell_draw(keys[7], (D, 6 * D), D ** -0.5, 0.1875, ((0, 128),)),
        "spatial_table": bell_draw(keys[8], (6, D), 0.5, 3.0, ((1, 128),)),
        "spatial_projection": bell_draw(keys[9], (D, 3 * D), D ** -0.5, 0.1875, ((0, 128),)),
        "spatial_output": bell_draw(keys[10], (D, D), (D // 12) ** -0.5, 0.625, ((0, 128),)),
        "spatial_up": bell_draw(keys[11], (D, FFN), D ** -0.5, 0.1875, ((0, 128),)),
        "spatial_down": bell_draw(keys[12], (FFN, D), FFN ** -0.5, 0.09375, ((0, 128),)),
        "temporal_table": bell_draw(keys[13], (6, D), 0.5, 3.0, ((1, 128),)),
        "temporal_projection": bell_draw(keys[14], (D, 3 * D), D ** -0.5, 0.1875, ((0, 128),)),
        "temporal_output": bell_draw(keys[15], (D, D), (D // 2) ** -0.5, 0.25, ((0, 128),)),
        "cross_query": bell_draw(keys[16], (D, D), D ** -0.5, 0.1875, ((0, 128),)),
        "cross_text": bell_draw(keys[17], (TEXT_DIM, 2 * D), TEXT_DIM ** -0.5, 0.09375, ((0, 128),)),
        "cross_output": bell_draw(keys[18], (D, D), (D // 8) ** -0.5, 0.5, ((0, 128),)),
        "cross_gain": jnp.clip(1.0 + 0.18 * jax.random.normal(keys[19], (D,), jnp.float32), 0.099609375, 1.8984375).astype(jnp.bfloat16),
        "temporal_up": bell_draw(keys[20], (D, FFN), D ** -0.5, 0.1875, ((0, 128),)),
        "temporal_down": bell_draw(keys[21], (FFN, D), FFN ** -0.5, 0.09375, ((0, 128),)),
    }


EPSILON = 1e-06
MASK_FILL = -1000000000.0
SPATIAL_FORMS = ('fphe,fqhe->fhpq', 'fhpq,fqhe->fphe')
TEMPORAL_FORMS = ('fphe,gphe->phfg', 'phfg,gphe->fphe')
CROSS_FORMS = ('fphe,lhe->fphl', 'fphl,lhe->fphe')

@jax.custom_vjp
def low(v):
    return lax.optimization_barrier(v.astype(jnp.bfloat16)).astype(jnp.float32)

@jax.custom_vjp
def low_back(v):
    return v

def low_keep(v):
    return (low(v), None)

def low_pass(kept, grad):
    return (grad,)

def back_keep(v):
    return (v, None)

def back_low(kept, grad):
    return (low(grad),)
low.defvjp(low_keep, low_pass)
low_back.defvjp(back_keep, back_low)

def matmul(operand, weight):
    return jnp.dot(operand, weight, precision=lax.Precision.HIGHEST)

def noise_table(count):
    beta_values = jnp.linspace(0.0001, 0.02, count, dtype=jnp.float32)
    return jnp.cumprod(1.0 - beta_values)

def time_features(timestep, feature_count):
    half_count = feature_count // 2
    frequency = jnp.exp(-math.log(10000.0) * jnp.arange(half_count, dtype=jnp.float32) / half_count)
    angles = timestep.astype(jnp.float32) * frequency
    return jnp.concatenate([jnp.cos(angles), jnp.sin(angles)])

def normalize(values):
    average = lax.optimization_barrier(jnp.mean(values, axis=-1, keepdims=True))
    centred = values - average
    return centred * lax.rsqrt(lax.optimization_barrier(jnp.mean(centred * centred, axis=-1, keepdims=True)) + EPSILON)

def attention(queries, key_rows, value_rows, einsum_forms, visible):
    factor = queries.shape[-1] ** (-0.5)
    scores = low_back(jnp.einsum(einsum_forms[0], queries, key_rows, precision=lax.Precision.HIGHEST) * factor)
    if visible is not None:
        scores = jnp.where(visible, scores, MASK_FILL)
    probability = low(jax.nn.softmax(scores, axis=-1))
    return low_back(low(jnp.einsum(einsum_forms[1], probability, value_rows, precision=lax.Precision.HIGHEST)))

def self_attention(hidden_state, modulation, projection, out_weight, einsum_forms):
    normed = low(normalize(hidden_state) * (1.0 + modulation[1]) + modulation[0])
    packed = low_back(low(matmul(normed, projection)))
    packed = packed.reshape(hidden_state.shape[:-1] + (3, HEADS, HEAD_DIM))
    mixed_rows = attention(packed[..., 0, :, :], packed[..., 1, :, :], packed[..., 2, :, :], einsum_forms, None)
    branch = low_back(matmul(mixed_rows.reshape(hidden_state.shape), out_weight))
    return hidden_state + modulation[2] * branch

def cross_attention(hidden_state, gain_vector, query_weight, text_keys, text_values, out_weight, visible):
    normed = low(normalize(hidden_state) * gain_vector)
    queries = low_back(low(matmul(normed, query_weight))).reshape(hidden_state.shape[:-1] + (HEADS, HEAD_DIM))
    mixed_rows = attention(queries, text_keys, text_values, CROSS_FORMS, visible)
    return hidden_state + low_back(matmul(mixed_rows.reshape(hidden_state.shape), out_weight))

def feed_forward(hidden_state, modulation, up_weight, down_weight):
    normed = low(normalize(hidden_state) * (1.0 + modulation[4]) + modulation[3])
    inner_rows = low_back(matmul(normed, up_weight))
    output = low_back(matmul(low(jax.nn.gelu(inner_rows, approximate=True)), down_weight))
    return hidden_state + modulation[5] * output

def forward_clip(latent_rows, noise_rows, timestep, text_rows, text_length, weights):
    time_input, time_output, spatial_table, spatial_projection, spatial_output, spatial_up, spatial_down, temporal_table, temporal_projection, temporal_output, cross_query, cross_text, cross_output, cross_gain, temporal_up, temporal_down = weights
    alpha_bar = noise_table(STEPS)[timestep]
    hidden_state = jnp.sqrt(alpha_bar) * latent_rows + jnp.sqrt(1.0 - alpha_bar) * noise_rows
    embedded = low(time_features(timestep, FREQ))
    pre_time = matmul(embedded, time_input)
    shared = matmul(low(jax.nn.silu(pre_time)), time_output).reshape(6, D)
    modulation = spatial_table + shared
    hidden_state = self_attention(hidden_state, modulation, spatial_projection, spatial_output, SPATIAL_FORMS)
    hidden_state = feed_forward(hidden_state, modulation, spatial_up, spatial_down)
    hidden_state = low_back(low(hidden_state))
    modulation = temporal_table + shared
    hidden_state = self_attention(hidden_state, modulation, temporal_projection, temporal_output, TEMPORAL_FORMS)
    projected = low_back(low(matmul(text_rows, cross_text)))
    text_keys = projected[:, :D].reshape(TEXT, HEADS, HEAD_DIM)
    text_values = projected[:, D:].reshape(TEXT, HEADS, HEAD_DIM)
    visible = jnp.arange(TEXT) < text_length
    hidden_state = cross_attention(hidden_state, cross_gain, cross_query, text_keys, text_values, cross_output, visible)
    return feed_forward(hidden_state, modulation, temporal_up, temporal_down)

def reference(latents, noise_sample, timesteps, text_states, text_lengths, cotangent, time_input, time_output, spatial_table, spatial_projection, spatial_output, spatial_up, spatial_down, temporal_table, temporal_projection, temporal_output, cross_query, cross_text, cross_output, cross_gain, temporal_up, temporal_down):
    params = tuple((weight.astype(jnp.float32) for weight in (time_input, time_output, spatial_table, spatial_projection, spatial_output, spatial_up, spatial_down, temporal_table, temporal_projection, temporal_output, cross_query, cross_text, cross_output, cross_gain, temporal_up, temporal_down)))

    def one_clip(totals, pieces):
        clip_latents, clip_noise, clip_step, clip_text, clip_length, clip_cotangent = pieces

        def forward(latent_rows, weights):
            return forward_clip(latent_rows, clip_noise.astype(jnp.float32), clip_step, clip_text.astype(jnp.float32), clip_length, weights)
        output, pullback = jax.vjp(forward, clip_latents.astype(jnp.float32), params)
        latent_part, weight_part = pullback(clip_cotangent.astype(jnp.float32))
        totals = tuple((running + fresh_grad for running, fresh_grad in zip(totals, weight_part)))
        return (totals, (output.astype(jnp.bfloat16), latent_part))
    zeros = tuple((jnp.zeros_like(weight) for weight in params))
    totals, (outputs, latent_grads) = lax.scan(one_clip, zeros, (latents, noise_sample, timesteps, text_states, text_lengths, cotangent))
    return (outputs, latent_grads, totals[0], totals[1], totals[2], totals[3], totals[4], totals[5], totals[6], totals[7], totals[8], totals[9], totals[10], totals[11], totals[12], totals[13], totals[14], totals[15])
```

```python
from functools import partial
import math

import jax
import jax.numpy as jnp
from jax import lax
from jax.sharding import Mesh, PartitionSpec as P

HEADS = 16
HEAD_DIM = 72
FREQ = 256
STEPS = 1000
D = 1152
FFN = 4608
EPSILON = 1e-06
MASK_FILL = -1000000000.0

CLIP = ("y", "z", "xl")
SEQ = ("xh", "c")
GROUP = ("xl", "xh", "c")
RING = ("xh", "xl")
ALL = ("y", "z", "xl", "xh", "c")
X_PLACE = (0, 2, 1, 3)

bf16 = jnp.bfloat16
f32 = jnp.float32

SPATIAL_FORMS = ("fphe,fqhe->fhpq", "fhpq,fqhe->fphe", "fhpq,fphe->fqhe")
TEMPORAL_FORMS = ("fphe,gphe->phfg", "phfg,gphe->fphe", "phfg,fphe->gphe")
CROSS_FORMS = ("fphe,lhe->fphl", "fphl,lhe->fphe", "fphl,fphe->lhe")


def fetch(value, axis, step):
    if axis == "x":
        pairs = [(X_PLACE[(i + step) % 4], X_PLACE[i]) for i in range(4)]
        return lax.ppermute(value, ("xl", "xh"), pairs)
    return lax.ppermute(value, axis, [((i + step) % 4, i) for i in range(4)])


def swap(value, axis):
    return lax.ppermute(value, axis, [(0, 1), (1, 0)])


def place_of(axis):
    if axis == "x":
        return lax.axis_index("xh") * 2 + lax.axis_index("xl")
    return lax.axis_index(axis)


def place(blocks, axis, pos):
    shape = blocks[0].shape
    out = jnp.zeros(shape[:pos] + (4,) + shape[pos:], blocks[0].dtype)
    own = place_of(axis)
    for step, block in enumerate(blocks):
        out = lax.dynamic_update_index_in_dim(out, block, lax.rem(own + step, 4), pos)
    return out


def place_down(blocks, axis):
    wide = []
    for block in blocks:
        halves = block.reshape(4, 2, 2, 72, 640)
        wide.append(jnp.concatenate([halves[:, :, 0], halves[:, :, 1, :, :512]], axis=3))
    return place(wide, axis, 1)


def ring_blocks(value, axis):
    return [value] + [fetch(value, axis, step) for step in (1, 3, 2)]


def in_order(blocks):
    return [blocks[0], blocks[1], blocks[3], blocks[2]]


def gather(value, axis, pos):
    return place(in_order(ring_blocks(value, axis)), axis, pos)


def pick(value, axis, step, pos):
    return lax.dynamic_index_in_dim(
        value, lax.rem(place_of(axis) + step, 4), pos, keepdims=False
    )


def scatter_sum(value, axis, pos):
    total = pick(value, axis, 0, pos).astype(f32)
    for step in (1, 3, 2):
        total = total + fetch(pick(value, axis, step, pos), axis, 4 - step).astype(f32)
    return total.astype(bf16)


def by_core(first, second, axis, dim):
    own_first = lax.axis_index(axis) == 0
    return jnp.concatenate(
        [jnp.where(own_first, first, second), jnp.where(own_first, second, first)], axis=dim
    )


def pair_sum(partial_rows):
    mine = partial_rows.astype(bf16)
    return mine.astype(f32) + swap(mine, "c").astype(f32)


def down_pairs(other):
    pairs = []
    for d in range(128):
        y1, y0, z1, z0 = (d >> 6) & 1, (d >> 5) & 1, (d >> 4) & 1, (d >> 3) & 1
        xl, xh, core = (d >> 2) & 1, (d >> 1) & 1, d & 1
        half = 1 - core if other else core
        target = 0
        for bit in (z0, xl, xh, half, z1, y0, y1):
            target = 2 * target + bit
        pairs.append((d, target))
    return pairs


def send_down(shards):
    core = lax.axis_index("c")
    low = shards[:, :, :640]
    high = jnp.pad(shards[:, :, 640:], ((0, 0), (0, 0), (0, 128)))
    first = lax.ppermute(jnp.where(core == 0, low, high), ALL, down_pairs(False))
    second = lax.ppermute(jnp.where(core == 0, high, low), ALL, down_pairs(True))
    half = lax.axis_index("z") % 2
    return jnp.concatenate(
        [jnp.where(half == 0, first, second), jnp.where(half == 0, second, first)], axis=1
    )


def return_down(blocks):
    half = lax.axis_index("z") % 2
    top, bottom = blocks[:, :36], blocks[:, 36:]
    back = [[(b, a) for a, b in down_pairs(other)] for other in (False, True)]
    first = lax.ppermute(jnp.where(half == 0, top, bottom), ALL, back[0])
    second = lax.ppermute(jnp.where(half == 0, bottom, top), ALL, back[1])
    core = lax.axis_index("c")
    low = jnp.where(core == 0, first, second)
    high = jnp.where(core == 0, second, first)
    return jnp.concatenate([low, high[:, :, :512]], axis=2)


def to_pieces(shard, groups):
    rows = shard.shape[0]
    value = shard.reshape(rows, groups, 2, 2, 2, -1)
    value = value.transpose(4, 3, 2, 0, 1, 5)
    return value.reshape(8, rows, -1)


def from_pieces(value, groups):
    rows = value.shape[1]
    value = value.reshape(2, 2, 2, rows, groups, -1)
    value = value.transpose(3, 4, 2, 1, 0, 5)
    return value.reshape(rows, -1)


def swap_group(value, axes):
    return lax.all_to_all(value, axes, split_axis=0, concat_axis=0, tiled=True)


def widen(value, width):
    return jnp.pad(value, [(0, 0)] * (value.ndim - 1) + [(0, width - value.shape[-1])])


def noise_table(count):
    beta_values = jnp.linspace(0.0001, 0.02, count, dtype=f32)
    return jnp.cumprod(1.0 - beta_values)


def time_features(timesteps, feature_count):
    half_count = feature_count // 2
    frequency = jnp.exp(-math.log(10000.0) * jnp.arange(half_count, dtype=f32) / half_count)
    angles = timesteps.astype(f32)[:, None] * frequency
    return jnp.concatenate([jnp.cos(angles), jnp.sin(angles)], axis=1)


def normalize(values):
    average = jnp.mean(values, axis=-1, keepdims=True)
    centred = values - average
    inverse_std = lax.rsqrt(jnp.mean(centred * centred, axis=-1, keepdims=True) + EPSILON)
    return (centred * inverse_std, inverse_std)


def norm_back(normal_rows, inverse_std, normal_grad):
    first_mean = jnp.mean(normal_grad, axis=-1, keepdims=True)
    second_mean = jnp.mean(normal_grad * normal_rows, axis=-1, keepdims=True)
    return inverse_std * (normal_grad - first_mean - normal_rows * second_mean)


def product(operand, weight):
    return jnp.dot(operand, weight, preferred_element_type=f32)


def product_back(operand, weight):
    return lax.dot_general(operand, weight, (((1,), (1,)), ((), ())), preferred_element_type=f32)


def outer_sum(operand, partner):
    return lax.dot_general(operand, partner, (((0,), (0,)), ((), ())), preferred_element_type=f32)


def attend_forward(queries, key_rows, value_rows, einsum_forms, visible):
    factor = HEAD_DIM ** (-0.5)
    scores = jnp.einsum(einsum_forms[0], queries, key_rows, preferred_element_type=f32) * factor
    if visible is not None:
        scores = jnp.where(visible, scores, MASK_FILL)
    row_max = jnp.max(scores, axis=-1, keepdims=True)
    exponent = jnp.exp(scores - row_max)
    denominator = jnp.sum(exponent, axis=-1, keepdims=True)
    probability = (exponent / denominator).astype(bf16)
    mixed_rows = jnp.einsum(einsum_forms[1], probability, value_rows, preferred_element_type=f32)
    return (mixed_rows.astype(bf16), row_max + jnp.log(denominator))


def attend_back(queries, key_rows, value_rows, mixed_grad, logsum, einsum_forms, visible):
    factor = HEAD_DIM ** (-0.5)
    scores = jnp.einsum(einsum_forms[0], queries, key_rows, preferred_element_type=f32) * factor
    if visible is not None:
        scores = jnp.where(visible, scores, MASK_FILL)
    probability = jnp.exp(scores - logsum)
    prob_grad = jnp.einsum(einsum_forms[0], mixed_grad, value_rows, preferred_element_type=f32)
    value_grad = jnp.einsum(
        einsum_forms[2], probability.astype(bf16), mixed_grad, preferred_element_type=f32
    )
    score_grad = probability * (
        prob_grad - jnp.sum(probability * prob_grad, axis=-1, keepdims=True)
    )
    score_grad = score_grad.astype(bf16)
    query_grad = (
        jnp.einsum(einsum_forms[1], score_grad, key_rows, preferred_element_type=f32) * factor
    )
    key_grad = (
        jnp.einsum(einsum_forms[2], score_grad, queries, preferred_element_type=f32) * factor
    )
    return (query_grad, key_grad, value_grad)


def both_columns(own):
    return by_core(own, swap(own, "c"), "c", 1)


def own_columns(value):
    half = value.shape[1] // 2
    return jnp.where(lax.axis_index("c") == 0, value[:, :half], value[:, half:])


def own_rows(value):
    half = value.shape[0] // 2
    return lax.dynamic_slice_in_dim(value, lax.axis_index("c") * half, half, 0)


def side_by_side(pieces, start, stop):
    return jnp.concatenate([pieces[j][:, start:stop] for j in range(4)], axis=1)


def heads_of(rows, lead):
    return rows.reshape(lead + (HEADS // 2, HEAD_DIM))


def attention_forward(hidden_state, modulation, weights, out_full, forms, lead):
    normal_rows, inverse_std = normalize(hidden_state)
    normed = (normal_rows * (1.0 + modulation[1]) + modulation[0]).astype(bf16)
    packed = [product(normed, weights[j]).astype(bf16) for j in range(4)]
    queries = heads_of(side_by_side(packed, 0, 144), lead)
    key_rows = heads_of(side_by_side(packed, 144, 288), lead)
    value_rows = heads_of(side_by_side(packed, 288, 432), lead)
    mixed_own, logsum = attend_forward(queries, key_rows, value_rows, forms, None)
    mixed_rows = both_columns(mixed_own.reshape(-1, D // 2))
    branch = product(mixed_rows, out_full)
    stored = (
        normal_rows,
        inverse_std,
        normed,
        queries,
        key_rows,
        value_rows,
        logsum,
        mixed_rows,
        branch,
    )
    return (hidden_state + modulation[2] * branch, stored)


def attention_back(incoming, stored, modulation, weights, out_full, forms):
    normal_rows, inverse_std, normed, queries, key_rows, value_rows, logsum, mixed_rows, branch = (
        stored
    )
    gate_grad = jnp.sum(incoming * branch, axis=0)
    branch_grad = (modulation[2] * incoming).astype(bf16)
    out_grad = outer_sum(mixed_rows, own_columns(branch_grad)).astype(bf16)
    mixed_grad = product_back(branch_grad, own_rows(out_full)).astype(bf16).reshape(queries.shape)
    parts = attend_back(queries, key_rows, value_rows, mixed_grad, logsum, forms, None)
    parts = [part.astype(bf16).reshape(-1, D // 2) for part in parts]
    packed_grad = [
        jnp.concatenate([part[:, 144 * j : 144 * j + 144] for part in parts], axis=1)
        for j in range(4)
    ]
    projection_grad = [outer_sum(normed, packed_grad[j]).astype(bf16) for j in range(4)]
    normed_grad = sum(product_back(packed_grad[j], weights[j][:, :432]) for j in range(4))
    normed_grad = pair_sum(normed_grad)
    scale_grad = jnp.sum(normed_grad * normal_rows, axis=0)
    shift_grad = jnp.sum(normed_grad, axis=0)
    upstream = incoming + norm_back(normal_rows, inverse_std, normed_grad * (1.0 + modulation[1]))
    return (upstream, projection_grad, out_grad, (shift_grad, scale_grad, gate_grad))


def cross_forward(hidden_state, gain_vector, query_weight, text_keys, text_values, out_full, visible, lead):
    normal_rows, inverse_std = normalize(hidden_state)
    normed = (normal_rows * gain_vector).astype(bf16)
    queries = heads_of(product(normed, query_weight).astype(bf16), lead)
    mixed_own, logsum = attend_forward(queries, text_keys, text_values, CROSS_FORMS, visible)
    mixed_rows = both_columns(mixed_own.reshape(-1, D // 2))
    branch = product(mixed_rows, out_full)
    return (hidden_state + branch, (normal_rows, inverse_std, normed, queries, logsum, mixed_rows))


def cross_back(incoming, stored, gain_vector, query_weight, text_keys, text_values, out_full, visible):
    normal_rows, inverse_std, normed, queries, logsum, mixed_rows = stored
    branch_grad = incoming.astype(bf16)
    out_grad = outer_sum(mixed_rows, own_columns(branch_grad)).astype(bf16)
    mixed_grad = product_back(branch_grad, own_rows(out_full)).astype(bf16).reshape(queries.shape)
    query_grad, key_grad, value_grad = attend_back(
        queries, text_keys, text_values, mixed_grad, logsum, CROSS_FORMS, visible
    )
    query_grad = query_grad.astype(bf16).reshape(-1, D // 2)
    query_weight_grad = outer_sum(normed, query_grad).astype(bf16)
    normed_grad = pair_sum(product_back(query_grad, query_weight))
    gain_grad = jnp.sum(normed_grad * normal_rows, axis=0)
    upstream = incoming + norm_back(normal_rows, inverse_std, normed_grad * gain_vector)
    key_grad = key_grad.reshape(key_grad.shape[0], -1)
    value_grad = value_grad.reshape(value_grad.shape[0], -1)
    return (upstream, gain_grad, query_weight_grad, out_grad, key_grad, value_grad)


def feed_forward(hidden_state, modulation, up_pieces, down):
    normal_rows, inverse_std = normalize(hidden_state)
    normed = (normal_rows * (1.0 + modulation[4]) + modulation[3]).astype(bf16)
    inner = [product(normed, up_pieces[j]) for j in range(4)]
    activated = [jax.nn.gelu(rows, approximate=True).astype(bf16)[:, :576] for rows in inner]
    activated = jnp.concatenate(activated, axis=1)
    output = pair_sum(product(activated, down))
    return (
        hidden_state + modulation[5] * output,
        (normal_rows, inverse_std, normed, inner, activated, output),
    )


def feed_forward_back(incoming, stored, modulation, up_pieces, down):
    normal_rows, inverse_std, normed, inner, activated, output = stored
    gate_grad = jnp.sum(incoming * output, axis=0)
    output_grad = (modulation[5] * incoming).astype(bf16)
    down_grad = outer_sum(activated, output_grad).astype(bf16)
    active_grad = product_back(output_grad, down)
    inner_grad = []
    for j in range(4):
        smooth_back = jax.vjp(partial(jax.nn.gelu, approximate=True), inner[j])[1]
        piece = widen(active_grad[:, 576 * j : 576 * j + 576], 640)
        inner_grad.append(smooth_back(piece)[0].astype(bf16))
    up_grad = jnp.stack([outer_sum(normed, inner_grad[j]).astype(bf16) for j in range(4)])
    normed_grad = pair_sum(sum(product_back(inner_grad[j], up_pieces[j]) for j in range(4)))
    scale_grad = jnp.sum(normed_grad * normal_rows, axis=0)
    shift_grad = jnp.sum(normed_grad, axis=0)
    upstream = incoming + norm_back(normal_rows, inverse_std, normed_grad * (1.0 + modulation[4]))
    return (upstream, up_grad, down_grad, (shift_grad, scale_grad, gate_grad))


def scatter_down(grad):
    grad = grad.reshape(4, 4, 2, 72, D)
    low, high = grad[..., :640], widen(grad[..., 640:], 640)
    grad = jnp.stack([low, high], axis=3)

    def part(step):
        return pick(grad, "y", step, 1).reshape(4, 4, 72, 640)

    total = part(0).astype(f32)
    for step in (1, 3, 2):
        total = total + fetch(part(step), "y", 4 - step).astype(f32)
    return scatter_sum(total.astype(bf16), "z", 1)


def local(
    latents,
    noise_sample,
    timesteps,
    text_states,
    text_lengths,
    cotangent,
    time_input,
    time_output,
    spatial_table,
    spatial_projection,
    spatial_output,
    spatial_up,
    spatial_down,
    temporal_table,
    temporal_projection,
    temporal_output,
    cross_query,
    cross_text,
    cross_output,
    cross_gain,
    temporal_up,
    temporal_down,
):
    core, far = lax.axis_index("c"), lax.axis_index("xh")
    clip = (lax.axis_index("y") * 4 + lax.axis_index("z")) * 2 + lax.axis_index("xl")
    me = clip * 4 + far * 2 + core

    sent = jnp.concatenate(
        [
            to_pieces(spatial_up, 1),
            to_pieces(spatial_projection, 3),
            to_pieces(spatial_output, 1),
            to_pieces(temporal_up, 1),
            to_pieces(temporal_projection, 3),
            to_pieces(temporal_output, 1),
            to_pieces(cross_query, 1),
            to_pieces(cross_output, 1),
        ],
        axis=2,
    )
    mine = swap_group(sent, GROUP).reshape(72, 2592)
    s_up = widen(mine[:, :576], 640)
    s_att = widen(mine[:, 576:1152], 640)
    t_up = widen(mine[:, 1152:1728], 640)
    t_att = widen(mine[:, 1728:2592], 896)
    downs = send_down(jnp.stack([spatial_down, temporal_down]))

    first_y = gather(jnp.concatenate([s_up, t_att], axis=1), "y", 0)
    first_x = gather(jnp.concatenate([s_att, downs[0], t_up, downs[1]], axis=1), "x", 0)

    s_up = gather(first_y[..., :640], "z", 1)
    s_up = lax.all_gather(s_up.reshape(D, 640), RING, axis=0, tiled=False)
    s_att = gather(gather(first_x[..., :640], "y", 1), "z", 2).reshape(4, D, 640)
    s_down = ring_blocks(gather(first_x[..., 640:1280], "z", 1), "y")
    s_down = place_down(in_order(s_down), "y").reshape(FFN // 2, D)

    t_att = gather(first_y[..., 640:], "z", 1)
    t_att = lax.all_gather(t_att.reshape(D, 896), RING, axis=0, tiled=False)
    t_up = gather(gather(first_x[..., 1280:1920], "y", 1), "z", 2).reshape(4, D, 640)
    t_down = ring_blocks(gather(first_x[..., 1920:], "z", 1), "y")
    t_down = place_down(in_order(t_down), "y").reshape(FFN // 2, D)

    words = cross_text.reshape(32, 2, 2, 2, 288).transpose(3, 2, 0, 1, 4).reshape(4, 32, 576)
    words = widen(swap_group(words, SEQ).reshape(128, 576), 640)
    words = by_core(words, swap(words, "xl"), "xl", 0)
    words = gather(words, "y", 0)
    words = lax.all_gather(words, "z", axis=0, tiled=False).reshape(4096, 640)

    split_steps = jnp.stack([timesteps // 32, timesteps % 32], axis=1).reshape(-1).astype(bf16)
    note = jnp.concatenate(
        [
            time_input.reshape(-1),
            spatial_table.reshape(-1),
            temporal_table.reshape(-1),
            cross_gain,
            split_steps,
            jnp.zeros((9,), bf16),
        ]
    )
    notes = swap_group(jnp.broadcast_to(note, (128, 2432)), ALL)
    full_time_input = notes[:, :2304].reshape(FREQ, D)
    tables = notes[:, 2304:2412].reshape(128, 12, 9).transpose(1, 0, 2).reshape(2, 6, D)
    full_gain = notes[:, 2412:2421].reshape(D).astype(f32)
    steps = notes[::4, 2421:2423].astype(f32)
    steps = (steps[:, 0] * 32.0 + steps[:, 1]).astype(jnp.int32)

    embedded = time_features(steps, FREQ).astype(bf16)
    pre_time = product(embedded, full_time_input)
    lifted = jax.nn.silu(pre_time).astype(bf16)
    own_lifted = lax.dynamic_slice_in_dim(lifted, me * 9, 9, 1)
    shares = swap_group(product(own_lifted, time_output).reshape(128, 1728), ALL)
    shared = jnp.sum(shares, axis=0)
    shared = by_core(shared, swap(shared, "c"), "c", 0)
    shared = by_core(shared, swap(shared, "xh"), "xh", 0).reshape(6, D)
    spatial_mod = tables[0].astype(f32) + shared
    temporal_mod = tables[1].astype(f32) + shared

    alpha_bars = noise_table(STEPS)
    picked = jnp.sum(jnp.where(jnp.arange(STEPS) == timesteps[0], alpha_bars, 0.0))
    signal_scale = jnp.sqrt(picked)

    frames = jnp.stack([latents[0, 0], noise_sample[0, 0]])
    other = swap(frames, "c")

    def noised(pair):
        return signal_scale * pair[0].astype(f32) + jnp.sqrt(1.0 - picked) * pair[1].astype(f32)

    hidden_state = by_core(noised(frames), noised(other), "c", 0)

    s_out = both_columns(side_by_side(s_att, 432, 576))
    hidden_state, spatial_attention = attention_forward(
        hidden_state, spatial_mod, s_att, s_out, SPATIAL_FORMS, (2, 160)
    )
    hidden_state, spatial_mlp = feed_forward(hidden_state, spatial_mod, s_up, s_down)

    def to_patches(rows):
        halves = rows.reshape(2, 2, 80, D)
        keep = lax.dynamic_index_in_dim(halves, far, 1, keepdims=False)
        give = lax.dynamic_index_in_dim(halves, 1 - far, 1, keepdims=False)
        return jnp.concatenate([keep, swap(give, "xh")], axis=0).reshape(320, D)

    patch_rows = to_patches(hidden_state.astype(bf16))
    own_cotangent = cotangent[0, 0]
    incoming = to_patches(by_core(own_cotangent, swap(own_cotangent, "c"), "c", 0)).astype(f32)

    text_order = text_states[0].reshape(120, 4, 4, 2, 128).transpose(0, 2, 1, 3, 4)
    text_order = text_order.reshape(120, 4096)
    text_rows = product(text_order, words)[:, :576].astype(bf16)
    other_text = swap(text_rows, "xh")
    text_keys = by_core(text_rows[:, :288], other_text[:, :288], "xh", 1).reshape(120, 8, 72)
    text_values = by_core(text_rows[:, 288:], other_text[:, 288:], "xh", 1).reshape(120, 8, 72)
    visible = jnp.arange(120) < text_lengths[0]

    t_out = both_columns(side_by_side(t_att, 432, 576))
    x_query = side_by_side(t_att, 576, 720)
    x_out = both_columns(side_by_side(t_att, 720, 864))
    hidden_state = patch_rows.astype(f32)
    hidden_state, temporal_attention = attention_forward(
        hidden_state, temporal_mod, t_att, t_out, TEMPORAL_FORMS, (4, 80)
    )
    hidden_state, cross_stored = cross_forward(
        hidden_state, full_gain, x_query, text_keys, text_values, x_out, visible, (4, 80)
    )
    hidden_state, temporal_mlp = feed_forward(hidden_state, temporal_mod, t_up, t_down)

    finished = hidden_state.astype(bf16).reshape(4, 80, D)
    keep = lax.dynamic_index_in_dim(finished, core, 0, keepdims=False)
    give = lax.dynamic_index_in_dim(finished, 2 + core, 0, keepdims=False)
    activations = by_core(keep, swap(give, "xh"), "xh", 0)[None, None]

    incoming, t_up_grad, t_down_grad, t_mlp_mod = feed_forward_back(
        incoming, temporal_mlp, temporal_mod, t_up, t_down
    )
    incoming, gain_grad, x_query_grad, x_out_grad, key_grad, value_grad = cross_back(
        incoming, cross_stored, full_gain, x_query, text_keys, text_values, x_out, visible
    )
    key_grad, value_grad = key_grad.astype(bf16), value_grad.astype(bf16)

    def text_half(which):
        def half(value):
            return lax.dynamic_slice_in_dim(value, which * 288, 288, 1)

        return jnp.concatenate([half(key_grad), half(value_grad)], axis=1)

    text_grad = text_half(far).astype(f32) + swap(text_half(1 - far), "xh").astype(f32)
    words_grad = outer_sum(text_order, widen(text_grad.astype(bf16), 640)).astype(bf16)
    words_grad = lax.psum_scatter(
        words_grad.reshape(4, 4 * 2 * 128, 640), "z", scatter_dimension=0, tiled=False
    )
    words_grad = scatter_sum(words_grad.reshape(4, 2, 128, 640), "y", 0)
    near = lax.axis_index("xl")
    words_grad = lax.dynamic_index_in_dim(words_grad, near, 0, keepdims=False).astype(f32) + swap(
        lax.dynamic_index_in_dim(words_grad, 1 - near, 0, keepdims=False), "xl"
    ).astype(f32)
    words_grad = swap_group(words_grad.astype(bf16)[:, :576].reshape(4, 32, 576), SEQ)
    words_grad = words_grad.reshape(2, 2, 32, 2, 288).transpose(2, 3, 1, 0, 4).reshape(32, 2304)

    incoming, t_proj_grad, t_out_grad, t_att_mod = attention_back(
        incoming, temporal_attention, temporal_mod, t_att, t_out, TEMPORAL_FORMS
    )
    t_mod_grad = jnp.stack(t_att_mod + t_mlp_mod)

    def piece(value, j):
        return value[:, 144 * j : 144 * j + 144]

    t_att_grad = jnp.stack(
        [
            widen(
                jnp.concatenate(
                    [t_proj_grad[j], piece(t_out_grad, j), piece(x_query_grad, j), piece(x_out_grad, j)],
                    axis=1,
                ),
                896,
            )
            for j in range(4)
        ]
    )

    def scatter_ring(grad):
        return lax.psum_scatter(grad, RING, scatter_dimension=0, tiled=False)

    def finish(up_grad, att_grad, down_grad):
        width = att_grad.shape[-1]
        if width == 640:
            ring, rest = up_grad, att_grad
        else:
            ring, rest = att_grad, up_grad
        down = scatter_down(down_grad)
        rest = scatter_sum(rest.reshape(4, 4, 4, 72, 640), "z", 2)
        rest = scatter_sum(rest, "y", 1)
        both = scatter_sum(jnp.concatenate([rest, down], axis=2), "x", 0)
        ring = scatter_ring(ring).reshape(4, 4, 72, -1)
        ring = scatter_sum(scatter_sum(ring, "z", 1), "y", 0)
        rest, down = both[:, :640], both[:, 640:]
        down = return_down(down[None])[0].astype(f32)
        up, att = (ring, rest) if width == 640 else (rest, ring)
        return up, att, down

    t_up_done, t_att_done, t_down_done = finish(t_up_grad, t_att_grad, t_down_grad)

    back = incoming.astype(bf16).reshape(4, 80, D)
    theirs = swap(back[2:], "xh")
    frame_grad = by_core(back[:2], theirs, "xh", 1).reshape(320, D).astype(f32)
    frame_grad, s_up_grad, s_down_grad, s_mlp_mod = feed_forward_back(
        frame_grad, spatial_mlp, spatial_mod, s_up, s_down
    )
    frame_grad, s_proj_grad, s_out_grad, s_att_mod = attention_back(
        frame_grad, spatial_attention, spatial_mod, s_att, s_out, SPATIAL_FORMS
    )
    latent_grad = signal_scale * lax.dynamic_index_in_dim(frame_grad.reshape(2, 160, D), core, 0)
    s_mod_grad = jnp.stack(s_att_mod + s_mlp_mod)
    s_att_grad = jnp.stack(
        [
            widen(jnp.concatenate([s_proj_grad[j], piece(s_out_grad, j)], axis=1), 640)
            for j in range(4)
        ]
    )
    s_up_done, s_att_done, s_down_done = finish(s_up_grad, s_att_grad, s_down_grad)

    returned = jnp.concatenate(
        [s_up_done[:, :576], s_att_done[:, :576], t_up_done[:, :576], t_att_done[:, :864]], axis=1
    )
    returned = swap_group(returned.reshape(8, 9, 2592), GROUP).astype(f32)
    s_up_grad = from_pieces(returned[..., :576], 1)
    s_proj_grad = from_pieces(returned[..., 576:1008], 3)
    s_out_grad = from_pieces(returned[..., 1008:1152], 1)
    t_up_grad = from_pieces(returned[..., 1152:1728], 1)
    t_proj_grad = from_pieces(returned[..., 1728:2160], 3)
    t_out_grad = from_pieces(returned[..., 2160:2304], 1)
    x_query_grad = from_pieces(returned[..., 2304:2448], 1)
    x_out_grad = from_pieces(returned[..., 2448:], 1)

    shared_grad = (s_mod_grad + t_mod_grad).reshape(4, 1728)
    shared_grad = shared_grad + swap(shared_grad, "xh")
    quarter = lax.dynamic_index_in_dim(shared_grad, far * 2 + core, 0, keepdims=False)
    table_part = jnp.stack([s_mod_grad, t_mod_grad]).reshape(12, 128, 9).transpose(1, 0, 2)
    table_part = jnp.concatenate([table_part.reshape(128, 108), gain_grad.reshape(128, 9)], axis=1)
    table_part = jnp.where(core == 0, table_part, 0.0)
    letter = jnp.concatenate(
        [jnp.broadcast_to(quarter, (128, 1728)), table_part, jnp.zeros((128, 75), f32)], axis=1
    )
    letters = swap_group(letter, ALL)
    all_shared = letters[:, :1728].reshape(32, 6 * D)
    table_sum = jnp.sum(letters[:, 1728:1845], axis=0)
    s_table_grad = table_sum[:54].reshape(6, 9)
    t_table_grad = table_sum[54:108].reshape(6, 9)
    cross_gain_grad = table_sum[108:]

    def exact(a, b, dims):
        return lax.dot_general(
            a, b, (dims, ((), ())), precision=lax.Precision.HIGHEST, preferred_element_type=f32
        )

    time_output_grad = exact(own_lifted.astype(f32), all_shared, ((0,), (0,)))
    lifted_grad = exact(all_shared, time_output.astype(f32), ((1,), (1,)))
    own_pre = lax.dynamic_slice_in_dim(pre_time, me * 9, 9, 1)
    own_pre_grad = jax.vjp(jax.nn.silu, own_pre)[1](lifted_grad)[0]
    card = jnp.broadcast_to(widen(own_pre_grad.reshape(288), 384), (128, 384))
    cards = swap_group(card, ALL)[:, :288].reshape(128, 32, 9)
    pre_grad = cards.transpose(1, 0, 2).reshape(32, D)
    own_embedded = lax.dynamic_slice_in_dim(embedded, me * 2, 2, 1).astype(f32)
    time_input_grad = exact(own_embedded, pre_grad, ((0,), (0,)))

    return (
        activations,
        latent_grad[None],
        time_input_grad,
        time_output_grad,
        s_table_grad,
        s_proj_grad,
        s_out_grad,
        s_up_grad,
        s_down_done,
        t_table_grad,
        t_proj_grad,
        t_out_grad,
        x_query_grad,
        words_grad.astype(f32),
        x_out_grad,
        cross_gain_grad,
        t_up_grad,
        t_down_done,
    )


def solution(mesh):
    fine = Mesh(mesh.devices.reshape(4, 4, 2, 2, 2), ALL)
    frames = P(CLIP, SEQ, None, None)
    rows = P(ALL, None)
    columns = P(None, ALL)
    in_specs = (
        frames,
        frames,
        P(CLIP),
        P(CLIP, None, None),
        P(CLIP),
        frames,
        rows,
        rows,
        columns,
        rows,
        rows,
        rows,
        rows,
        columns,
        rows,
        rows,
        rows,
        rows,
        rows,
        P(ALL),
        rows,
        rows,
    )
    out_specs = (
        frames,
        frames,
        rows,
        rows,
        columns,
        rows,
        rows,
        rows,
        rows,
        columns,
        rows,
        rows,
        rows,
        rows,
        rows,
        P(ALL),
        rows,
        rows,
    )
    return jax.shard_map(local, mesh=fine, in_specs=in_specs, out_specs=out_specs, check_vma=False)
```

```python
from functools import partial
import math

import jax
import jax.numpy as jnp
from jax import lax
from jax.experimental import pallas as pl
from jax.experimental.pallas import tpu as pltpu
from jax.sharding import Mesh, PartitionSpec as P

HEADS = 16
HEAD_DIM = 72
FREQ = 256
STEPS = 1000
D = 1152
FFN = 4608
EPSILON = 1e-06
MASK_FILL = -1000000000.0

CLIP = ("y", "z", "xl")
SEQ = ("xh", "c")
GROUP = ("xl", "xh", "c")
RING = ("xh", "xl")
ALL = ("y", "z", "xl", "xh", "c")
X_PLACE = (0, 2, 1, 3)

bf16 = jnp.bfloat16
f32 = jnp.float32


def fetch(value, axis, step):
    if axis == "x":
        pairs = [(X_PLACE[(i + step) % 4], X_PLACE[i]) for i in range(4)]
        return lax.ppermute(value, ("xl", "xh"), pairs)
    return lax.ppermute(value, axis, [((i + step) % 4, i) for i in range(4)])


def swap(value, axis):
    return lax.ppermute(value, axis, [(0, 1), (1, 0)])


def place_of(axis):
    if axis == "x":
        return lax.axis_index("xh") * 2 + lax.axis_index("xl")
    return lax.axis_index(axis)


def turn(step, row, which, rows):
    return jnp.where(step == which, row, jnp.where(step < which, 0, rows - 1))


def place_kernel(widths, own_ref, *refs):
    blocks, outs = refs[:4], refs[4:]
    for which in range(4):

        @pl.when(pl.program_id(0) == which)
        def _():
            start = 0
            for width, out in zip(widths, outs):
                out[...] = blocks[which][..., start : start + width].reshape(out.shape)
                start += width


def place(blocks, axis, pos, widths):
    lead, last = blocks[0].shape[:pos], blocks[0].shape[pos:]
    rows = math.prod(lead)
    group = min(rows, 4)
    rows //= group
    flat = [block.reshape((rows, group) + last) for block in blocks]
    zeros = (0,) * len(last)
    whole = (group,) + last

    def in_map(which):
        return lambda step, row, own: (turn(step, row, which, rows), 0) + zeros

    def out_map(step, row, own):
        return (row, 0, lax.rem(own[0] + step, 4)) + zeros

    outs = pl.pallas_call(
        partial(place_kernel, widths),
        out_shape=[
            jax.ShapeDtypeStruct((rows, group, 4) + last[:-1] + (width,), bf16) for width in widths
        ],
        grid_spec=pltpu.PrefetchScalarGridSpec(
            num_scalar_prefetch=1,
            grid=(4, rows),
            in_specs=[pl.BlockSpec((1,) + whole, in_map(which)) for which in range(4)],
            out_specs=[
                pl.BlockSpec((1, group, 1) + last[:-1] + (width,), out_map) for width in widths
            ],
        ),
        compiler_params=pltpu.CompilerParams(vmem_limit_bytes=40 * 2**20),
        cost_estimate=pl.CostEstimate(flops=0, bytes_accessed=0, transcendentals=0),
    )(place_of(axis).reshape(1), *flat)
    return [out.reshape(lead + out.shape[2:]) for out in outs]


def ring_blocks(value, axis):
    return [value] + [fetch(value, axis, step) for step in (1, 3, 2)]


def in_order(blocks):
    return [blocks[0], blocks[1], blocks[3], blocks[2]]


def after(values, earlier):
    return lax.optimization_barrier((values, earlier))[0]


def fetch_rings(jobs, earlier):
    values = after([value for value, _ in jobs], earlier)
    blocks = [[value] for value, _ in jobs]
    for step in (1, 3, 2):
        for n, (_, axis) in enumerate(jobs):
            blocks[n].append(fetch(values[n], axis, step))
    blocks = lax.optimization_barrier(blocks)
    return [in_order(own) for own in blocks], [own[1] for own in blocks]


def sum_rings(jobs, earlier):
    sent = [
        [pick(value, axis, step, pos) for step in (1, 3, 2)] for value, axis, pos in jobs
    ]
    sent = after(sent, earlier)
    arrived = [
        [fetch(own[k], axis, 4 - step) for k, step in enumerate((1, 3, 2))]
        for own, (_, axis, _) in zip(sent, jobs)
    ]
    arrived = lax.optimization_barrier(arrived)
    totals = []
    for own, (value, axis, pos) in zip(arrived, jobs):
        total = pick(value, axis, 0, pos).astype(f32)
        for block in own:
            total = total + block.astype(f32)
        totals.append(total.astype(bf16))
    return totals, [own[0] for own in arrived]


def pick(value, axis, step, pos):
    return lax.dynamic_index_in_dim(
        value, lax.rem(place_of(axis) + step, 4), pos, keepdims=False
    )


def by_core(first, second, axis, dim):
    own_first = lax.axis_index(axis) == 0
    return jnp.concatenate(
        [jnp.where(own_first, first, second), jnp.where(own_first, second, first)], axis=dim
    )


def down_pairs(other):
    pairs = []
    for d in range(128):
        y1, y0, z1, z0 = (d >> 6) & 1, (d >> 5) & 1, (d >> 4) & 1, (d >> 3) & 1
        xl, xh, core = (d >> 2) & 1, (d >> 1) & 1, d & 1
        half = 1 - core if other else core
        target = 0
        for bit in (z0, xl, xh, half, z1, y0, y1):
            target = 2 * target + bit
        pairs.append((d, target))
    return pairs


def send_down(shards):
    core = lax.axis_index("c")
    low = shards[:, :, :640]
    high = jnp.pad(shards[:, :, 640:], ((0, 0), (0, 0), (0, 128)))
    first = lax.ppermute(jnp.where(core == 0, low, high), ALL, down_pairs(False))
    second = lax.ppermute(jnp.where(core == 0, high, low), ALL, down_pairs(True))
    half = lax.axis_index("z") % 2
    return jnp.concatenate(
        [jnp.where(half == 0, first, second), jnp.where(half == 0, second, first)], axis=1
    )


def return_down(blocks):
    half = lax.axis_index("z") % 2
    top, bottom = blocks[:, :36], blocks[:, 36:]
    back = [[(b, a) for a, b in down_pairs(other)] for other in (False, True)]
    first = lax.ppermute(jnp.where(half == 0, top, bottom), ALL, back[0])
    second = lax.ppermute(jnp.where(half == 0, bottom, top), ALL, back[1])
    core = lax.axis_index("c")
    low = jnp.where(core == 0, first, second)
    high = jnp.where(core == 0, second, first)
    return jnp.concatenate([low, high[:, :, :512]], axis=2)


def to_pieces(shard, groups):
    rows = shard.shape[0]
    value = shard.reshape(rows, groups, 2, 2, 2, -1)
    value = value.transpose(4, 3, 2, 0, 1, 5)
    return value.reshape(8, rows, -1)


def from_pieces(value, groups):
    rows = value.shape[1]
    value = value.reshape(2, 2, 2, rows, groups, -1)
    value = value.transpose(3, 4, 2, 1, 0, 5)
    return value.reshape(rows, -1)


def swap_group(value, axes):
    return lax.all_to_all(value, axes, split_axis=0, concat_axis=0, tiled=True)


def widen(value, width):
    return jnp.pad(value, [(0, 0)] * (value.ndim - 1) + [(0, width - value.shape[-1])])


def noise_table(count):
    beta_values = jnp.linspace(0.0001, 0.02, count, dtype=f32)
    return jnp.cumprod(1.0 - beta_values)


def time_features(timesteps, feature_count):
    half_count = feature_count // 2
    frequency = jnp.exp(-math.log(10000.0) * jnp.arange(half_count, dtype=f32) / half_count)
    angles = timesteps.astype(f32)[:, None] * frequency
    return jnp.concatenate([jnp.cos(angles), jnp.sin(angles)], axis=1)


def normalize(values):
    average = jnp.mean(values, axis=-1, keepdims=True)
    centred = values - average
    inverse_std = lax.rsqrt(jnp.mean(centred * centred, axis=-1, keepdims=True) + EPSILON)
    return (centred * inverse_std, inverse_std)


def norm_back(normal_rows, inverse_std, normal_grad):
    first_mean = jnp.mean(normal_grad, axis=-1, keepdims=True)
    second_mean = jnp.mean(normal_grad * normal_rows, axis=-1, keepdims=True)
    return inverse_std * (normal_grad - first_mean - normal_rows * second_mean)


def product(operand, weight):
    return jnp.dot(operand, weight, preferred_element_type=f32)


def product_back(operand, weight):
    return lax.dot_general(operand, weight, (((1,), (1,)), ((), ())), preferred_element_type=f32)


def outer_sum(operand, partner):
    return lax.dot_general(operand, partner, (((0,), (0,)), ((), ())), preferred_element_type=f32)


def apart(own):
    other = swap(own, "c")
    first = lax.axis_index("c") == 0
    low, high = jnp.where(first, own, other), jnp.where(first, other, own)
    return jnp.concatenate([low[j] for j in range(4)] + [high[j] for j in range(4)], axis=1)


def windows(value, start):
    rows = value.shape[0]
    pieces = jnp.swapaxes(value.reshape(rows, 4, 144), 0, 1)
    return jnp.pad(pieces, ((0, 0), (0, 0), (start, 112 - start)))


def norm_value(values):
    centred = values - jnp.mean(values, axis=-1, keepdims=True)
    return centred * lax.rsqrt(jnp.mean(centred * centred, axis=-1, keepdims=True) + EPSILON)


def softmax_value(queries, keys, bias):
    scores = product_back(queries, keys) * HEAD_DIM ** (-0.5)
    if bias is not None:
        scores = scores + bias
    exponent = jnp.exp(scores - jnp.max(scores, axis=-1, keepdims=True))
    return exponent / jnp.sum(exponent, axis=-1, keepdims=True)


def head_back(queries, keys, values, mixed_grad, bias):
    factor = HEAD_DIM ** (-0.5)
    probability = softmax_value(queries, keys, bias)
    prob_grad = product_back(mixed_grad, values)
    value_grad = outer_sum(probability.astype(bf16), mixed_grad)
    inner = jnp.sum(probability * prob_grad, axis=-1, keepdims=True)
    score_grad = (probability * (prob_grad - inner)).astype(bf16)
    return product(score_grad, keys) * factor, outer_sum(score_grad, queries) * factor, value_grad


def whole(shape):
    return pl.BlockSpec(shape, lambda j: (0,) * len(shape))


def part(shape):
    return pl.BlockSpec((1,) + shape, lambda j: (j,) + (0,) * len(shape))


def shaped(shape, dtype=bf16):
    return jax.ShapeDtypeStruct(shape, dtype)


def by_piece(kernel, out_shape, in_specs, out_specs, scratch, args):
    return pl.pallas_call(
        kernel,
        out_shape=out_shape,
        grid=(4,),
        in_specs=in_specs,
        out_specs=out_specs,
        scratch_shapes=scratch,
        compiler_params=pltpu.CompilerParams(vmem_limit_bytes=48 * 2**20),
        cost_estimate=pl.CostEstimate(flops=0, bytes_accessed=0, transcendentals=0),
    )(*args)


def first_piece(action):
    pl.when(pl.program_id(0) == 0)(action)


def last_piece(action):
    pl.when(pl.program_id(0) == 3)(action)


def self_kernel(groups, x_ref, shift_ref, scale_ref, weight_ref, *refs):
    bias_ref = refs[0] if groups == 1 else None
    normed_ref, packed_ref, mixed_ref = refs[-3:]

    @first_piece
    def _():
        normed = norm_value(x_ref[...]) * (1.0 + scale_ref[...]) + shift_ref[...]
        normed_ref[...] = normed.astype(bf16)

    packed = product(normed_ref[...], weight_ref[0]).astype(bf16)
    packed_ref[0] = packed
    rows = 320 // groups
    for group in range(groups):
        mixed = []
        for head in range(2):
            queries, keys, values = (
                packed[group * rows : group * rows + rows, start : start + 72]
                for start in (72 * head, 144 + 72 * head, 288 + 72 * head)
            )
            bias = None if bias_ref is None else bias_ref[...]
            probability = softmax_value(queries, keys, bias).astype(bf16)
            mixed.append(product(probability, values))
        mixed_ref[0, group * rows : group * rows + rows, :] = jnp.concatenate(
            mixed, axis=1
        ).astype(bf16)


def self_forward(groups, hidden_state, shift, scale, weights, bias):
    specs = [whole((320, D)), whole((1, D)), whole((1, D)), part((D, 640))]
    args = [hidden_state, shift[None], scale[None], weights]
    if groups == 1:
        specs.append(whole((320, 320)))
        args.append(bias)
    return by_piece(
        partial(self_kernel, groups),
        [shaped((320, D)), shaped((4, 320, 640)), shaped((4, 320, 144))],
        specs,
        [whole((320, D)), part((320, 640)), part((320, 144))],
        [],
        args,
    )


def self_back_kernel(groups, extras, *refs):
    packed_ref, mixed_grad_ref, weight_ref, normed_ref = refs[:4]
    pairs = refs[4 : 4 + 2 * extras]
    bias_ref = refs[4 + 2 * extras] if groups == 1 else None
    grad_ref, normed_grad_ref, total_ref = refs[-3:]
    packed, mixed_grad = packed_ref[0], mixed_grad_ref[0]
    rows = 320 // groups
    strips = []
    for group in range(groups):
        at = group * rows
        parts = []
        for head in range(2):
            queries, keys, values = (
                packed[at : at + rows, start : start + 72]
                for start in (72 * head, 144 + 72 * head, 288 + 72 * head)
            )
            bias = None if bias_ref is None else bias_ref[...]
            own_grad = mixed_grad[at : at + rows, 72 * head : 72 * head + 72]
            parts.append(head_back(queries, keys, values, own_grad, bias))
        line = [parts[head][which] for which in range(3) for head in range(2)]
        line.append(jnp.zeros((rows, 208), f32))
        strips.append(jnp.concatenate(line, axis=1).astype(bf16))
    packed_grad = strips[0] if groups == 1 else jnp.concatenate(strips, axis=0)
    width = weight_ref.shape[2]
    grad = outer_sum(normed_ref[...], packed_grad)
    if width > 640:
        grad = jnp.concatenate([grad, jnp.zeros((D, width - 640), f32)], axis=1)
    for n in range(extras):
        start = (384, 512, 640)[n]
        own = outer_sum(pairs[2 * n][...], pairs[2 * n + 1][0])
        lines = [grad[:, :start], grad[:, start : start + 256] + own, grad[:, start + 256 :]]
        grad = jnp.concatenate([line for line in lines if line.shape[1] > 0], axis=1)
    grad_ref[0] = grad.astype(bf16)
    back = product_back(packed_grad, weight_ref[0, :, :640])

    @first_piece
    def _():
        total_ref[...] = back

    @pl.when(pl.program_id(0) > 0)
    def _():
        total_ref[...] += back

    @last_piece
    def _():
        normed_grad_ref[...] = total_ref[...].astype(bf16)


def self_back(groups, packed, mixed_grad, weights, normed, pairs, bias):
    width = weights.shape[-1]
    specs = [part((320, 640)), part((320, 144)), part((D, width)), whole((320, D))]
    args = [packed, mixed_grad, weights, normed]
    for rows, window in pairs:
        specs += [whole((320, D)), part((320, 256))]
        args += [rows, window]
    if groups == 1:
        specs.append(whole((320, 320)))
        args.append(bias)
    return by_piece(
        partial(self_back_kernel, groups, len(pairs)),
        [shaped((4, D, width)), shaped((320, D))],
        specs,
        [part((D, width)), whole((320, D))],
        [pltpu.VMEM((320, D), f32)],
        args,
    )


def out_kernel(start, mixed_ref, weight_ref, out_ref):
    low = start // 128 * 128
    value = product(mixed_ref[...], weight_ref[0, :, low : low + 256])
    out_ref[0] = value[:, start - low : start - low + 144].astype(bf16)


def out_forward(mixed_rows, weights, start):
    return by_piece(
        partial(out_kernel, start),
        shaped((4, 320, 144)),
        [whole((320, D)), part(weights.shape[1:])],
        part((320, 144)),
        [],
        [mixed_rows, weights],
    )


def out_back_kernel(low, window_ref, weight_ref, out_ref, total_ref):
    back = product_back(window_ref[0], weight_ref[0, :, low : low + 256])

    @first_piece
    def _():
        total_ref[...] = back

    @pl.when(pl.program_id(0) > 0)
    def _():
        total_ref[...] += back

    @last_piece
    def _():
        for n in range(8):
            out_ref[n] = total_ref[:, 144 * n : 144 * n + 144].astype(bf16)


def out_back(window, weights, low):
    halves = by_piece(
        partial(out_back_kernel, low),
        shaped((8, 320, 144)),
        [part((320, 256)), part(weights.shape[1:])],
        whole((8, 320, 144)),
        [pltpu.VMEM((320, D), f32)],
        [window, weights],
    ).reshape(2, 4, 320, 144)
    core = lax.axis_index("c")
    keep = lax.dynamic_index_in_dim(halves, core, 0, keepdims=False)
    give = lax.dynamic_index_in_dim(halves, 1 - core, 0, keepdims=False)
    return (keep.astype(f32) + swap(give, "c").astype(f32)).astype(bf16)


def cross_kernel(x_ref, gain_ref, weight_ref, key_ref, value_ref, bias_ref, normed_ref, query_ref, mixed_ref):
    @first_piece
    def _():
        normed_ref[...] = (norm_value(x_ref[...]) * gain_ref[...]).astype(bf16)

    queries = product(normed_ref[...], weight_ref[0, :, :256]).astype(bf16)[:, 64:208]
    query_ref[0] = queries
    keys, values = key_ref[0], value_ref[0]
    mixed = []
    for head in range(2):
        own = slice(72 * head, 72 * head + 72)
        probability = softmax_value(queries[:, own], keys[:, own], bias_ref[...])
        mixed.append(product(probability.astype(bf16), values[:, own]))
    mixed_ref[0] = jnp.concatenate(mixed, axis=1).astype(bf16)


def cross_forward(hidden_state, gain, weights, keys, values, bias):
    return by_piece(
        cross_kernel,
        [shaped((320, D)), shaped((4, 320, 144)), shaped((4, 320, 144))],
        [whole((320, D)), whole((1, D)), part((D, 384))]
        + [part((128, 144)), part((128, 144)), whole((1, 128))],
        [whole((320, D)), part((320, 144)), part((320, 144))],
        [],
        [hidden_state, gain[None], weights, keys, values, bias],
    )


def cross_back_kernel(
    query_ref, key_ref, value_ref, grad_ref, weight_ref, bias_ref, window_ref, key_out, value_out, normed_ref, total_ref
):
    queries, keys, values, mixed_grad = query_ref[0], key_ref[0], value_ref[0], grad_ref[0]
    parts = []
    for head in range(2):
        own = slice(72 * head, 72 * head + 72)
        parts.append(
            head_back(queries[:, own], keys[:, own], values[:, own], mixed_grad[:, own], bias_ref[...])
        )
    zeros = jnp.zeros((320, 64), f32)
    window = jnp.concatenate(
        [zeros, parts[0][0], parts[1][0], zeros[:, :48]], axis=1
    ).astype(bf16)
    window_ref[0] = window
    key_out[0] = jnp.concatenate([parts[0][1], parts[1][1]], axis=1).astype(bf16)
    value_out[0] = jnp.concatenate([parts[0][2], parts[1][2]], axis=1).astype(bf16)
    back = product_back(window, weight_ref[0, :, :256])

    @first_piece
    def _():
        total_ref[...] = back

    @pl.when(pl.program_id(0) > 0)
    def _():
        total_ref[...] += back

    @last_piece
    def _():
        normed_ref[...] = total_ref[...].astype(bf16)


def cross_back(queries, keys, values, mixed_grad, weights, bias):
    return by_piece(
        cross_back_kernel,
        [shaped((4, 320, 256)), shaped((4, 128, 144)), shaped((4, 128, 144)), shaped((320, D))],
        [part((320, 144)), part((128, 144)), part((128, 144)), part((320, 144)), part((D, 384)), whole((1, 128))],
        [part((320, 256)), part((128, 144)), part((128, 144)), whole((320, D))],
        [pltpu.VMEM((320, D), f32)],
        [queries, keys, values, mixed_grad, weights, bias],
    )


GELU_SCALE = math.sqrt(2.0 / math.pi)


def down_halves(down_ref):
    blocks = [(y, 2 * z) for y in range(4) for z in range(2)]
    low = jnp.concatenate([down_ref[0, y, z] for y, z in blocks], axis=0)
    high = jnp.concatenate([down_ref[0, y, z + 1, :, :512] for y, z in blocks], axis=0)
    return low, high


def feed_kernel(x_ref, shift_ref, scale_ref, up_ref, down_ref, normed_ref, inner_ref, active_ref, out_ref, total_ref):
    @first_piece
    def _():
        normed = norm_value(x_ref[...]) * (1.0 + scale_ref[...]) + shift_ref[...]
        normed_ref[...] = normed.astype(bf16)

    inner = product(normed_ref[...], up_ref[0])
    inner_ref[0] = inner
    bent = jnp.tanh(GELU_SCALE * (inner + 0.044715 * inner * inner * inner))
    active = (0.5 * inner * (1.0 + bent)).astype(bf16)[:, :576]
    active_ref[0] = active
    low, high = down_halves(down_ref)

    @first_piece
    def _():
        total_ref[:, :640] = product(active, low)
        total_ref[:, 640:] = product(active, high)

    @pl.when(pl.program_id(0) > 0)
    def _():
        total_ref[:, :640] += product(active, low)
        total_ref[:, 640:] += product(active, high)

    @last_piece
    def _():
        out_ref[...] = total_ref[...].astype(bf16)


def feed_forward(hidden_state, shift, scale, up, down):
    return by_piece(
        feed_kernel,
        [shaped((320, D)), shaped((4, 320, 640), f32), shaped((4, 320, 576)), shaped((320, D))],
        [whole((320, D)), whole((1, D)), whole((1, D)), part((D, 640)), part((4, 4, 72, 640))],
        [whole((320, D)), part((320, 640)), part((320, 576)), whole((320, D))],
        [pltpu.VMEM((320, D), f32)],
        [hidden_state, shift[None], scale[None], up, down],
    )


def feed_back_kernel(
    grad_ref, inner_ref, active_ref, normed_ref, up_ref, down_ref, up_out, down_out, normed_grad_ref, total_ref
):
    low, high = down_halves(down_ref)
    low_grad, high_grad = grad_ref[:, :640], grad_ref[:, 640:]
    low_out = outer_sum(active_ref[0], low_grad).astype(bf16)
    high_out = outer_sum(active_ref[0], high_grad).astype(bf16)
    for block in range(8):
        rows = slice(72 * block, 72 * block + 72)
        down_out[0, block // 2, block % 2 * 2] = low_out[rows]
        down_out[0, block // 2, block % 2 * 2 + 1, :, :512] = high_out[rows]
        down_out[0, block // 2, block % 2 * 2 + 1, :, 512:] = jnp.zeros((72, 128), bf16)
    inner = inner_ref[0]
    active_grad = product_back(low_grad, low) + product_back(high_grad, high)
    active_grad = jnp.concatenate([active_grad, jnp.zeros((320, 64), f32)], axis=1)
    square = inner * inner
    bent = jnp.tanh(GELU_SCALE * inner * (1.0 + 0.044715 * square))
    slope = 0.5 * (1.0 + bent) + 0.5 * inner * (1.0 - bent * bent) * GELU_SCALE * (
        1.0 + 0.134145 * square
    )
    inner_grad = (active_grad * slope).astype(bf16)
    up_out[0] = outer_sum(normed_ref[...], inner_grad).astype(bf16)
    back = product_back(inner_grad, up_ref[0])

    @first_piece
    def _():
        total_ref[...] = back

    @pl.when(pl.program_id(0) > 0)
    def _():
        total_ref[...] += back

    @last_piece
    def _():
        normed_grad_ref[...] = total_ref[...].astype(bf16)


def feed_back(output_grad, inner, active, normed, up, down):
    return by_piece(
        feed_back_kernel,
        [shaped((4, D, 640)), shaped((4, 4, 4, 72, 640)), shaped((320, D))],
        [whole((320, D)), part((320, 640)), part((320, 576)), whole((320, D))]
        + [part((D, 640)), part((4, 4, 72, 640))],
        [part((D, 640)), part((4, 4, 72, 640)), whole((320, D))],
        [pltpu.VMEM((320, D), f32)],
        [output_grad, inner, active, normed, up, down],
    )


def both_cores(partial_rows):
    return partial_rows.astype(f32) + swap(partial_rows, "c").astype(f32)


def attention_block(groups, hidden_state, modulation, weights, bias):
    normed, packed, mixed = self_forward(
        groups, hidden_state, modulation[0], modulation[1], weights, bias
    )
    mixed_rows = apart(mixed)
    branch = apart(out_forward(mixed_rows, weights, 432)).astype(f32)
    stored = (hidden_state, normed, packed, mixed_rows, branch)
    return (hidden_state + modulation[2] * branch, stored)


def attention_block_back(groups, incoming, stored, modulation, weights, pairs, bias, earlier):
    hidden_state, normed, packed, mixed_rows, branch = stored
    gate_grad = jnp.sum(incoming * branch, axis=0)
    branch_grad = (modulation[2] * incoming).astype(bf16)
    window = windows(own_columns(branch_grad), 48)
    mixed_grad = after(out_back(window, weights, 384), earlier)
    weight_grad, normed_grad = self_back(
        groups, packed, mixed_grad, weights, normed, [(mixed_rows, window)] + pairs, bias
    )
    normed_grad = both_cores(normed_grad)
    normal_rows, inverse_std = normalize(hidden_state)
    scale_grad = jnp.sum(normed_grad * normal_rows, axis=0)
    shift_grad = jnp.sum(normed_grad, axis=0)
    upstream = incoming + norm_back(normal_rows, inverse_std, normed_grad * (1.0 + modulation[1]))
    return (upstream, weight_grad, (shift_grad, scale_grad, gate_grad))


def feed_block(hidden_state, modulation, up, down):
    normed, inner, active, output = feed_forward(
        hidden_state, modulation[3], modulation[4], up, down
    )
    output = both_cores(output)
    return (hidden_state + modulation[5] * output, (hidden_state, normed, inner, active, output))


def feed_block_back(incoming, stored, modulation, up, down):
    hidden_state, normed, inner, active, output = stored
    gate_grad = jnp.sum(incoming * output, axis=0)
    output_grad = (modulation[5] * incoming).astype(bf16)
    up_grad, down_grad, normed_grad = feed_back(output_grad, inner, active, normed, up, down)
    normed_grad = both_cores(normed_grad)
    normal_rows, inverse_std = normalize(hidden_state)
    scale_grad = jnp.sum(normed_grad * normal_rows, axis=0)
    shift_grad = jnp.sum(normed_grad, axis=0)
    upstream = incoming + norm_back(normal_rows, inverse_std, normed_grad * (1.0 + modulation[4]))
    return (upstream, up_grad, down_grad, (shift_grad, scale_grad, gate_grad))


def scatter_ring(grad):
    return lax.psum_scatter(grad, RING, scatter_dimension=0, tiled=False)


def own_columns(value):
    half = value.shape[1] // 2
    return jnp.where(lax.axis_index("c") == 0, value[:, :half], value[:, half:])


def local(
    latents,
    noise_sample,
    timesteps,
    text_states,
    text_lengths,
    cotangent,
    time_input,
    time_output,
    spatial_table,
    spatial_projection,
    spatial_output,
    spatial_up,
    spatial_down,
    temporal_table,
    temporal_projection,
    temporal_output,
    cross_query,
    cross_text,
    cross_output,
    cross_gain,
    temporal_up,
    temporal_down,
):
    core, far = lax.axis_index("c"), lax.axis_index("xh")
    clip = (lax.axis_index("y") * 4 + lax.axis_index("z")) * 2 + lax.axis_index("xl")
    me = clip * 4 + far * 2 + core

    sent = jnp.concatenate(
        [
            to_pieces(spatial_up, 1),
            to_pieces(spatial_projection, 3),
            to_pieces(spatial_output, 1),
            to_pieces(temporal_up, 1),
            to_pieces(temporal_projection, 3),
            to_pieces(temporal_output, 1),
            to_pieces(cross_query, 1),
            to_pieces(cross_output, 1),
        ],
        axis=2,
    )
    words = cross_text.reshape(4, 8, 2, 2, 2, 288).transpose(4, 3, 1, 0, 2, 5).reshape(4, 8, 2304)
    words = jnp.pad(words, ((0, 0), (0, 1), (0, 0)))
    near = lax.axis_index("xl")
    words = jnp.stack([jnp.where(near == 0, words, 0), jnp.where(near == 1, words, 0)])
    sent = jnp.concatenate([sent, words.reshape(8, 9, 2304)], axis=2)
    mine = swap_group(sent, GROUP)
    words = lax.dynamic_slice_in_dim(mine[:, :8, 2592:], near * 4, 4, 0)
    words = words.reshape(4, 8, 4, 576).transpose(0, 2, 1, 3).reshape(128, 576)
    words = widen(words, 640)
    mine = mine[..., :2592].reshape(72, 2592)
    shards = jnp.stack([spatial_down, temporal_down])
    s_up = widen(mine[:, :576], 640)
    s_att = widen(mine[:, 576:1152], 640)
    t_up = widen(mine[:, 1152:1728], 640)
    t_att = widen(mine[:, 1728:2592], 896)
    downs = send_down(shards)

    split_steps = jnp.stack([timesteps // 32, timesteps % 32], axis=1).reshape(-1).astype(bf16)
    note = jnp.concatenate(
        [
            time_input.reshape(-1),
            spatial_table.reshape(-1),
            temporal_table.reshape(-1),
            cross_gain,
            split_steps,
            jnp.zeros((9,), bf16),
        ]
    )
    notes = swap_group(jnp.broadcast_to(note, (128, 2432)), ALL)
    full_time_input = notes[:, :2304].reshape(FREQ, D)

    near_words = by_core(words, swap(words, "xl"), "xl", 0)
    rings, first_done = fetch_rings(
        [
            (jnp.concatenate([s_up, t_att, s_att], axis=1), "y"),
            (jnp.concatenate([downs[0], downs[1], t_up], axis=1), "z"),
        ],
        (),
    )
    up_att, s_att = place(rings[0], "y", 0, (1536, 640))
    s_down, down_up = place(rings[1], "z", 0, (640, 1280))
    rings, second_done = fetch_rings(
        [
            (up_att, "z"),
            (jnp.concatenate([s_att, s_down], axis=2), "x"),
            (down_up, "y"),
            (near_words, "y"),
        ],
        (first_done, full_time_input),
    )
    steps = notes[::4, 2421:2423].astype(f32)
    steps = (steps[:, 0] * 32.0 + steps[:, 1]).astype(jnp.int32)
    embedded = time_features(steps, FREQ).astype(bf16)
    pre_time = product(embedded, full_time_input)
    lifted = jax.nn.silu(pre_time).astype(bf16)
    own_lifted = lax.dynamic_slice_in_dim(lifted, me * 9, 9, 1)
    shares = after(product(own_lifted, time_output), first_done)
    shares = swap_group(shares.reshape(128, 1728), ALL)
    shares, rings = lax.optimization_barrier((shares, rings))
    s_up, t_att = place(rings[0], "z", 1, (640, 896))
    s_att, s_down = place(rings[1], "x", 0, (640, 640))
    t_down, t_up = place(rings[2], "y", 0, (640, 640))
    (words,) = place(rings[3], "y", 0, (640,))
    t_att = lax.all_gather(t_att.reshape(D, 896), RING, axis=0, tiled=False)
    words = lax.all_gather(words.reshape(1024, 640), "z", axis=0, tiled=False).reshape(4096, 640)
    t_up = lax.all_gather(t_up.reshape(D, 640), RING, axis=0, tiled=False)
    t_down = lax.all_gather(t_down.reshape(D, 640), RING, axis=0, tiled=False)
    t_down = t_down.reshape(4, 4, 4, 72, 640)

    tables = notes[:, 2304:2412].reshape(128, 12, 9).transpose(1, 0, 2).reshape(2, 6, D)
    full_gain = notes[:, 2412:2421].reshape(D).astype(f32)
    shared = jnp.sum(shares, axis=0)
    shared = by_core(shared, swap(shared, "c"), "c", 0)
    shared = by_core(shared, swap(shared, "xh"), "xh", 0).reshape(6, D)
    rings, _ = fetch_rings([(s_att, "z"), (s_down, "y"), (s_up, "x")], (second_done, shared))
    (s_att,) = place(rings[0], "z", 2, (640,))
    s_att = s_att.reshape(4, D, 640)
    (s_down,) = place(rings[1], "y", 1, (640,))
    (s_up,) = place(rings[2], "x", 0, (640,))
    s_up = s_up.reshape(4, D, 640)

    spatial_mod = tables[0].astype(f32) + shared
    temporal_mod = tables[1].astype(f32) + shared

    alpha_bars = noise_table(STEPS)
    picked = jnp.sum(jnp.where(jnp.arange(STEPS) == timesteps[0], alpha_bars, 0.0))
    signal_scale = jnp.sqrt(picked)

    frames = jnp.stack([latents[0, 0], noise_sample[0, 0]])
    other = swap(frames, "c")

    def noised(pair):
        return signal_scale * pair[0].astype(f32) + jnp.sqrt(1.0 - picked) * pair[1].astype(f32)

    hidden_state = by_core(noised(frames), noised(other), "c", 0)

    hidden_state, spatial_attention = attention_block(2, hidden_state, spatial_mod, s_att, None)
    hidden_state, spatial_mlp = feed_block(hidden_state, spatial_mod, s_up, s_down)

    def to_patches(rows):
        halves = rows.reshape(2, 2, 80, D)
        keep = lax.dynamic_index_in_dim(halves, far, 1, keepdims=False)
        give = lax.dynamic_index_in_dim(halves, 1 - far, 1, keepdims=False)
        return jnp.concatenate([keep, swap(give, "xh")], axis=0).reshape(320, D)

    patch_rows = to_patches(hidden_state.astype(bf16))
    own_cotangent = cotangent[0, 0]
    incoming = to_patches(by_core(own_cotangent, swap(own_cotangent, "c"), "c", 0)).astype(f32)

    text_order = text_states[0].reshape(120, 4, 4, 2, 128).transpose(0, 2, 1, 3, 4)
    text_order = text_order.reshape(120, 4096)
    text_rows = product(text_order, words)[:, :576].astype(bf16)
    other_text = swap(text_rows, "xh")
    def text_pieces(value):
        pieces = jnp.swapaxes(value.reshape(120, 4, 144), 0, 1)
        return jnp.pad(pieces, ((0, 0), (0, 8), (0, 0)))

    text_keys = text_pieces(by_core(text_rows[:, :288], other_text[:, :288], "xh", 1))
    text_values = text_pieces(by_core(text_rows[:, 288:], other_text[:, 288:], "xh", 1))
    text_bias = jnp.where(jnp.arange(128) < text_lengths[0], 0.0, MASK_FILL)[None]
    row = jnp.arange(320) % 80
    patch_bias = jnp.where(row[:, None] == row[None], 0.0, MASK_FILL)

    t_cross = t_att[..., 512:]
    hidden_state = patch_rows.astype(f32)
    hidden_state, temporal_attention = attention_block(
        1, hidden_state, temporal_mod, t_att, patch_bias
    )
    cross_state = hidden_state
    cross_normed, cross_queries, cross_mixed = cross_forward(
        cross_state, full_gain, t_cross, text_keys, text_values, text_bias
    )
    cross_mixed = apart(cross_mixed)
    hidden_state = cross_state + apart(out_forward(cross_mixed, t_cross, 208)).astype(f32)
    hidden_state, temporal_mlp = feed_block(hidden_state, temporal_mod, t_up, t_down)

    finished = hidden_state.astype(bf16).reshape(4, 80, D)
    keep = lax.dynamic_index_in_dim(finished, core, 0, keepdims=False)
    give = lax.dynamic_index_in_dim(finished, 2 + core, 0, keepdims=False)
    activations = by_core(keep, swap(give, "xh"), "xh", 0)[None, None]

    incoming, t_up_grad, t_down_grad, t_mlp_mod = feed_block_back(
        incoming, temporal_mlp, temporal_mod, t_up, t_down
    )
    t_up_grad = scatter_ring(t_up_grad).reshape(4, 4, 72, 640)
    t_down_grad = scatter_ring(t_down_grad.reshape(4, D, 640)).reshape(4, 4, 72, 640)
    cross_grad = incoming.astype(bf16)
    out_window = windows(own_columns(cross_grad), 80)
    cross_mixed_grad = out_back(out_window, t_cross, 128)
    query_window, key_grad, value_grad, normed_grad = cross_back(
        cross_queries, text_keys, text_values, cross_mixed_grad, t_cross, text_bias
    )
    normed_grad = both_cores(normed_grad)
    normal_rows, inverse_std = normalize(cross_state)
    gain_grad = jnp.sum(normed_grad * normal_rows, axis=0)
    incoming = incoming + norm_back(normal_rows, inverse_std, normed_grad * full_gain)
    key_grad = jnp.swapaxes(key_grad[:, :120], 0, 1).reshape(120, 576)
    value_grad = jnp.swapaxes(value_grad[:, :120], 0, 1).reshape(120, 576)

    def text_half(which):
        def half(value):
            return lax.dynamic_slice_in_dim(value, which * 288, 288, 1)

        return jnp.concatenate([half(key_grad), half(value_grad)], axis=1)

    text_grad = text_half(far).astype(f32) + swap(text_half(1 - far), "xh").astype(f32)
    words_grad = outer_sum(text_order, widen(text_grad.astype(bf16), 640)).astype(bf16)
    words_grad = words_grad.reshape(4, 1024, 640)
    words_grad = lax.psum_scatter(words_grad, "z", scatter_dimension=0, tiled=False)
    words_grad = words_grad.reshape(4, 256, 640)
    words_grad = lax.psum_scatter(words_grad, "y", scatter_dimension=0, tiled=False)
    words_grad = words_grad.reshape(2, 128, 640)
    words_grad = lax.dynamic_index_in_dim(words_grad, near, 0, keepdims=False).astype(f32) + swap(
        lax.dynamic_index_in_dim(words_grad, 1 - near, 0, keepdims=False), "xl"
    ).astype(f32)
    words_grad = words_grad.astype(bf16)

    incoming, t_att_grad, t_att_mod = attention_block_back(
        1,
        incoming,
        temporal_attention,
        temporal_mod,
        t_att,
        [(cross_normed, query_window), (cross_mixed, out_window)],
        patch_bias,
        text_grad,
    )
    t_mod_grad = jnp.stack(t_att_mod + t_mlp_mod)

    back = incoming.astype(bf16).reshape(4, 80, D)
    theirs = swap(back[2:], "xh")
    t_att_grad = scatter_ring(t_att_grad).reshape(4, 4, 72, 896)


    frame_grad = by_core(back[:2], theirs, "xh", 1).reshape(320, D).astype(f32)
    frame_grad, s_up_grad, s_down_grad, s_mlp_mod = feed_block_back(
        frame_grad, spatial_mlp, spatial_mod, s_up, s_down
    )
    s_up_grad = s_up_grad.reshape(4, 4, 4, 72, 640)
    (s_up_grad, s_down_grad), s_done = sum_rings(
        [(s_up_grad, "z", 2), (s_down_grad, "y", 1)], ()
    )
    frame_grad, s_att_grad, s_att_mod = attention_block_back(
        2, frame_grad, spatial_attention, spatial_mod, s_att, [], None, s_done
    )
    latent_grad = signal_scale * lax.dynamic_index_in_dim(frame_grad.reshape(2, 160, D), core, 0)
    s_mod_grad = jnp.stack(s_att_mod + s_mlp_mod)
    s_att_grad = s_att_grad.reshape(4, 4, 4, 72, 640)
    (att_x_y, att_x_z, att_y_z), done = sum_rings(
        [
            (s_att_grad[..., :256], "z", 2),
            (s_att_grad[..., 256:512], "y", 1),
            (s_att_grad[..., 512:], "x", 0),
        ],
        (),
    )
    up_att = jnp.concatenate([t_up_grad, t_att_grad], axis=3)
    down_att = jnp.concatenate([t_down_grad, att_y_z], axis=3)
    up_x_y = jnp.concatenate([s_up_grad, att_x_y], axis=3)
    down_x_z = jnp.concatenate([s_down_grad, att_x_z], axis=3)
    (up_att, down_att, up_x_y, down_x_z), done = sum_rings(
        [(up_att, "z", 1), (down_att, "y", 0), (up_x_y, "y", 1), (down_x_z, "x", 0)], done
    )
    down = jnp.concatenate([down_att, down_x_z], axis=2)
    (up_att, down, up_x), done = sum_rings(
        [(up_att, "y", 0), (down, "z", 0), (up_x_y, "x", 0)], done
    )
    downs = return_down(jnp.stack([down[:, 768:1408], down[:, :640]])).astype(f32)
    s_down_done, t_down_done = downs[0], downs[1]
    words_grad = swap_group(words_grad[:, :576].reshape(4, 32, 576), SEQ)
    words_grad = words_grad.reshape(2, 2, 32, 2, 288).transpose(2, 3, 1, 0, 4).reshape(32, 2304)

    returned = jnp.concatenate(
        [
            up_x[:, :576],
            up_x[:, 640:],
            down[:, 1408:],
            down[:, 640:704],
            up_att[:, :576],
            up_att[:, 640:1504],
        ],
        axis=1,
    )
    returned = swap_group(returned.reshape(8, 9, 2592), GROUP).astype(f32)
    s_up_grad = from_pieces(returned[..., :576], 1)
    s_proj_grad = from_pieces(returned[..., 576:1008], 3)
    s_out_grad = from_pieces(returned[..., 1008:1152], 1)
    t_up_grad = from_pieces(returned[..., 1152:1728], 1)
    t_proj_grad = from_pieces(returned[..., 1728:2160], 3)
    t_out_grad = from_pieces(returned[..., 2160:2304], 1)
    x_query_grad = from_pieces(returned[..., 2304:2448], 1)
    x_out_grad = from_pieces(returned[..., 2448:], 1)

    shared_grad = (s_mod_grad + t_mod_grad).reshape(4, 1728)
    shared_grad = shared_grad + swap(shared_grad, "xh")
    quarter = lax.dynamic_index_in_dim(shared_grad, far * 2 + core, 0, keepdims=False)
    table_part = jnp.stack([s_mod_grad, t_mod_grad]).reshape(12, 128, 9).transpose(1, 0, 2)
    table_part = jnp.concatenate([table_part.reshape(128, 108), gain_grad.reshape(128, 9)], axis=1)
    table_part = jnp.where(core == 0, table_part, 0.0)
    letter = jnp.concatenate(
        [jnp.broadcast_to(quarter, (128, 1728)), table_part, jnp.zeros((128, 75), f32)], axis=1
    )
    letters = swap_group(letter, ALL)
    all_shared = letters[:, :1728].reshape(32, 6 * D)
    table_sum = jnp.sum(letters[:, 1728:1845], axis=0)
    s_table_grad = table_sum[:54].reshape(6, 9)
    t_table_grad = table_sum[54:108].reshape(6, 9)
    cross_gain_grad = table_sum[108:]

    def exact(a, b, dims):
        return lax.dot_general(
            a, b, (dims, ((), ())), precision=lax.Precision.HIGHEST, preferred_element_type=f32
        )

    time_output_grad = exact(own_lifted.astype(f32), all_shared, ((0,), (0,)))
    lifted_grad = exact(all_shared, time_output.astype(f32), ((1,), (1,)))
    own_pre = lax.dynamic_slice_in_dim(pre_time, me * 9, 9, 1)
    own_pre_grad = jax.vjp(jax.nn.silu, own_pre)[1](lifted_grad)[0]
    card = jnp.broadcast_to(widen(own_pre_grad.reshape(288), 384), (128, 384))
    cards = swap_group(card, ALL)[:, :288].reshape(128, 32, 9)
    pre_grad = cards.transpose(1, 0, 2).reshape(32, D)
    own_embedded = lax.dynamic_slice_in_dim(embedded, me * 2, 2, 1).astype(f32)
    time_input_grad = exact(own_embedded, pre_grad, ((0,), (0,)))

    return (
        activations,
        latent_grad[None],
        time_input_grad,
        time_output_grad,
        s_table_grad,
        s_proj_grad,
        s_out_grad,
        s_up_grad,
        s_down_done,
        t_table_grad,
        t_proj_grad,
        t_out_grad,
        x_query_grad,
        words_grad.astype(f32),
        x_out_grad,
        cross_gain_grad,
        t_up_grad,
        t_down_done,
    )


def solution(mesh):
    fine = Mesh(mesh.devices.reshape(4, 4, 2, 2, 2), ALL)
    frames = P(CLIP, SEQ, None, None)
    rows = P(ALL, None)
    columns = P(None, ALL)
    in_specs = (
        frames,
        frames,
        P(CLIP),
        P(CLIP, None, None),
        P(CLIP),
        frames,
        rows,
        rows,
        columns,
        rows,
        rows,
        rows,
        rows,
        columns,
        rows,
        rows,
        rows,
        rows,
        rows,
        P(ALL),
        rows,
        rows,
    )
    out_specs = (
        frames,
        frames,
        rows,
        rows,
        columns,
        rows,
        rows,
        rows,
        rows,
        columns,
        rows,
        rows,
        rows,
        rows,
        rows,
        P(ALL),
        rows,
        rows,
    )
    return jax.shard_map(local, mesh=fine, in_specs=in_specs, out_specs=out_specs, check_vma=False)
```

```python
from functools import partial
import math

import jax
import jax.numpy as jnp
from jax import lax
from jax.experimental import pallas as pl
from jax.experimental.pallas import tpu as pltpu
from jax.sharding import Mesh, PartitionSpec as P

HEADS = 16
HEAD_DIM = 72
FREQ = 256
STEPS = 1000
D = 1152
FFN = 4608
EPSILON = 1e-06
MASK_FILL = -1000000000.0

CLIP = ("y", "z", "xl")
SEQ = ("xh", "c")
GROUP = ("xl", "xh", "c")
RING = ("xh", "xl")
ALL = ("y", "z", "xl", "xh", "c")
X_PLACE = (0, 2, 1, 3)

bf16 = jnp.bfloat16
f32 = jnp.float32


def fetch(value, axis, step):
    if axis == "x":
        pairs = [(X_PLACE[(i + step) % 4], X_PLACE[i]) for i in range(4)]
        return lax.ppermute(value, ("xl", "xh"), pairs)
    return lax.ppermute(value, axis, [((i + step) % 4, i) for i in range(4)])


def swap(value, axis):
    return lax.ppermute(value, axis, [(0, 1), (1, 0)])


def place_of(axis):
    if axis == "x":
        return lax.axis_index("xh") * 2 + lax.axis_index("xl")
    return lax.axis_index(axis)


def turn(step, row, which, rows):
    return jnp.where(step == which, row, jnp.where(step < which, 0, rows - 1))


def place_kernel(widths, own_ref, *refs):
    blocks, outs = refs[:4], refs[4:]
    for which in range(4):

        @pl.when(pl.program_id(0) == which)
        def _():
            start = 0
            for width, out in zip(widths, outs):
                out[...] = blocks[which][..., start : start + width].reshape(out.shape)
                start += width


def place(blocks, axis, pos, widths):
    lead, last = blocks[0].shape[:pos], blocks[0].shape[pos:]
    rows = math.prod(lead)
    group = min(rows, 4)
    rows //= group
    flat = [block.reshape((rows, group) + last) for block in blocks]
    zeros = (0,) * len(last)
    whole = (group,) + last

    def in_map(which):
        return lambda step, row, own: (turn(step, row, which, rows), 0) + zeros

    def out_map(step, row, own):
        return (row, 0, lax.rem(own[0] + step, 4)) + zeros

    outs = pl.pallas_call(
        partial(place_kernel, widths),
        out_shape=[
            jax.ShapeDtypeStruct((rows, group, 4) + last[:-1] + (width,), bf16) for width in widths
        ],
        grid_spec=pltpu.PrefetchScalarGridSpec(
            num_scalar_prefetch=1,
            grid=(4, rows),
            in_specs=[pl.BlockSpec((1,) + whole, in_map(which)) for which in range(4)],
            out_specs=[
                pl.BlockSpec((1, group, 1) + last[:-1] + (width,), out_map) for width in widths
            ],
        ),
        compiler_params=pltpu.CompilerParams(vmem_limit_bytes=40 * 2**20),
        cost_estimate=pl.CostEstimate(flops=0, bytes_accessed=0, transcendentals=0),
    )(place_of(axis).reshape(1), *flat)
    return [out.reshape(lead + out.shape[2:]) for out in outs]


def ring_blocks(value, axis):
    return [value] + [fetch(value, axis, step) for step in (1, 3, 2)]


def in_order(blocks):
    return [blocks[0], blocks[1], blocks[3], blocks[2]]


def after(values, earlier):
    return lax.optimization_barrier((values, earlier))[0]


def tie_kernel(*refs):
    pass


def tie(value, *earlier):
    anywhere = pl.BlockSpec(memory_space=pl.ANY)
    return pl.pallas_call(
        tie_kernel,
        out_shape=jax.ShapeDtypeStruct(value.shape, value.dtype),
        in_specs=[anywhere] * (1 + len(earlier)),
        out_specs=anywhere,
        input_output_aliases={0: 0},
        cost_estimate=pl.CostEstimate(flops=0, bytes_accessed=0, transcendentals=0),
    )(value, *earlier)


def fetch_rings(jobs, earlier):
    values = after([value for value, _ in jobs], earlier)
    blocks = [[value] for value, _ in jobs]
    for step in (1, 3, 2):
        for n, (_, axis) in enumerate(jobs):
            blocks[n].append(fetch(values[n], axis, step))
    blocks = lax.optimization_barrier(blocks)
    return [in_order(own) for own in blocks], [own[1] for own in blocks]


def gather_rings(jobs, earlier):
    values = after([value for value, _ in jobs], earlier)
    near = [(fetch(v, axis, 1), fetch(v, axis, 3)) for v, (_, axis) in zip(values, jobs)]
    near = lax.optimization_barrier(near)
    half = [value.shape[0] // 2 for value in values]
    across = [
        (fetch(up[:h], axis, 1), fetch(down[h:], axis, 3))
        for (up, down), h, (_, axis) in zip(near, half, jobs)
    ]
    near, across = lax.optimization_barrier((near, across))
    blocks = [
        [value, up, jnp.concatenate(pair, axis=0), down]
        for (value, _), (up, down), pair in zip(jobs, near, across)
    ]
    return blocks, [pair[0] for pair in across]


def ring_block(parts, axis, step):
    blocks = [pick(value, axis, step, pos) for value, pos in parts]
    return blocks[0] if len(blocks) == 1 else jnp.concatenate(blocks, axis=-1)


def add(*values):
    total = values[0].astype(f32)
    for value in values[1:]:
        total = total + value.astype(f32)
    return total.astype(bf16)


def sum_rings(jobs, earlier):
    sent = [[ring_block(parts, axis, step) for step in (1, 3, 2)] for parts, axis in jobs]
    sent = after(sent, earlier)
    arrived = [
        [fetch(own[k], axis, 4 - step) for k, step in enumerate((1, 3, 2))]
        for own, (_, axis) in zip(sent, jobs)
    ]
    arrived = lax.optimization_barrier(arrived)
    totals = [add(ring_block(parts, axis, 0), *own) for own, (parts, axis) in zip(arrived, jobs)]
    return totals, [own[0] for own in arrived]


def scatter_rings(jobs, earlier):
    sent = after([ring_block(parts, axis, 2) for parts, axis in jobs], earlier)
    half = [value.shape[0] // 2 for value in sent]
    across = [
        (fetch(value[:h], axis, 3), fetch(value[h:], axis, 1))
        for value, h, (_, axis) in zip(sent, half, jobs)
    ]
    across = lax.optimization_barrier(across)
    near = []
    for (low, high), h, (parts, axis) in zip(across, half, jobs):
        up, down = ring_block(parts, axis, 1), ring_block(parts, axis, 3)
        up = jnp.concatenate([add(up[:h], low), up[h:]], axis=0)
        down = jnp.concatenate([down[:h], add(down[h:], high)], axis=0)
        near.append((up, down))
    near = lax.optimization_barrier(near)
    near = [
        (fetch(up, axis, 3), fetch(down, axis, 1)) for (up, down), (_, axis) in zip(near, jobs)
    ]
    near = lax.optimization_barrier(near)
    totals = [add(ring_block(parts, axis, 0), *pair) for pair, (parts, axis) in zip(near, jobs)]
    return totals, [pair[0] for pair in across], [pair[0] for pair in near]


def pick(value, axis, step, pos):
    return lax.dynamic_index_in_dim(
        value, lax.rem(place_of(axis) + step, 4), pos, keepdims=False
    )


def by_core(first, second, axis, dim):
    own_first = lax.axis_index(axis) == 0
    return jnp.concatenate(
        [jnp.where(own_first, first, second), jnp.where(own_first, second, first)], axis=dim
    )


def down_pairs(other):
    pairs = []
    for d in range(128):
        y1, y0, z1, z0 = (d >> 6) & 1, (d >> 5) & 1, (d >> 4) & 1, (d >> 3) & 1
        xl, xh, core = (d >> 2) & 1, (d >> 1) & 1, d & 1
        half = 1 - core if other else core
        target = 0
        for bit in (z0, xl, xh, half, z1, y0, y1):
            target = 2 * target + bit
        pairs.append((d, target))
    return pairs


def send_down(shards):
    core = lax.axis_index("c")
    low = shards[:, :, :640]
    high = jnp.pad(shards[:, :, 640:], ((0, 0), (0, 0), (0, 128)))
    first = lax.ppermute(jnp.where(core == 0, low, high), ALL, down_pairs(False))
    second = lax.ppermute(jnp.where(core == 0, high, low), ALL, down_pairs(True))
    half = lax.axis_index("z") % 2
    return jnp.concatenate(
        [jnp.where(half == 0, first, second), jnp.where(half == 0, second, first)], axis=1
    )


def return_down(blocks):
    half = lax.axis_index("z") % 2
    top, bottom = blocks[:, :36], blocks[:, 36:]
    back = [[(b, a) for a, b in down_pairs(other)] for other in (False, True)]
    first = lax.ppermute(jnp.where(half == 0, top, bottom), ALL, back[0])
    second = lax.ppermute(jnp.where(half == 0, bottom, top), ALL, back[1])
    core = lax.axis_index("c")
    low = jnp.where(core == 0, first, second)
    high = jnp.where(core == 0, second, first)
    return jnp.concatenate([low, high[:, :, :512]], axis=2)


def to_pieces(shard, groups):
    rows = shard.shape[0]
    value = shard.reshape(rows, groups, 2, 2, 2, -1)
    value = value.transpose(4, 3, 2, 0, 1, 5)
    return value.reshape(8, rows, -1)


def from_pieces(value, groups):
    rows = value.shape[1]
    value = value.reshape(2, 2, 2, rows, groups, -1)
    value = value.transpose(3, 4, 2, 1, 0, 5)
    return value.reshape(rows, -1)


def swap_group(value, axes):
    return lax.all_to_all(value, axes, split_axis=0, concat_axis=0, tiled=True)


def widen(value, width):
    return jnp.pad(value, [(0, 0)] * (value.ndim - 1) + [(0, width - value.shape[-1])])


def noise_table(count):
    beta_values = jnp.linspace(0.0001, 0.02, count, dtype=f32)
    return jnp.cumprod(1.0 - beta_values)


def time_features(timesteps, feature_count):
    half_count = feature_count // 2
    frequency = jnp.exp(-math.log(10000.0) * jnp.arange(half_count, dtype=f32) / half_count)
    angles = timesteps.astype(f32)[:, None] * frequency
    return jnp.concatenate([jnp.cos(angles), jnp.sin(angles)], axis=1)


def normalize(values):
    average = jnp.mean(values, axis=-1, keepdims=True)
    centred = values - average
    inverse_std = lax.rsqrt(jnp.mean(centred * centred, axis=-1, keepdims=True) + EPSILON)
    return (centred * inverse_std, inverse_std)


def norm_back(normal_rows, inverse_std, normal_grad):
    first_mean = jnp.mean(normal_grad, axis=-1, keepdims=True)
    second_mean = jnp.mean(normal_grad * normal_rows, axis=-1, keepdims=True)
    return inverse_std * (normal_grad - first_mean - normal_rows * second_mean)


def product(operand, weight):
    return jnp.dot(operand, weight, preferred_element_type=f32)


def product_back(operand, weight):
    return lax.dot_general(operand, weight, (((1,), (1,)), ((), ())), preferred_element_type=f32)


def outer_sum(operand, partner):
    return lax.dot_general(operand, partner, (((0,), (0,)), ((), ())), preferred_element_type=f32)


def apart(own):
    other = swap(own, "c")
    first = lax.axis_index("c") == 0
    low, high = jnp.where(first, own, other), jnp.where(first, other, own)
    return jnp.concatenate([low[j] for j in range(4)] + [high[j] for j in range(4)], axis=1)


def windows(value, start):
    rows = value.shape[0]
    pieces = jnp.swapaxes(value.reshape(rows, 4, 144), 0, 1)
    return jnp.pad(pieces, ((0, 0), (0, 0), (start, 112 - start)))


def norm_value(values):
    centred = values - jnp.mean(values, axis=-1, keepdims=True)
    return centred * lax.rsqrt(jnp.mean(centred * centred, axis=-1, keepdims=True) + EPSILON)


def softmax_value(queries, keys, bias):
    scores = product_back(queries, keys) * HEAD_DIM ** (-0.5)
    if bias is not None:
        scores = scores + bias
    exponent = jnp.exp(scores - jnp.max(scores, axis=-1, keepdims=True))
    return exponent / jnp.sum(exponent, axis=-1, keepdims=True)


def head_back(queries, keys, values, mixed_grad, bias):
    factor = HEAD_DIM ** (-0.5)
    probability = softmax_value(queries, keys, bias)
    prob_grad = product_back(mixed_grad, values)
    value_grad = outer_sum(probability.astype(bf16), mixed_grad)
    inner = jnp.sum(probability * prob_grad, axis=-1, keepdims=True)
    score_grad = (probability * (prob_grad - inner)).astype(bf16)
    return product(score_grad, keys) * factor, outer_sum(score_grad, queries) * factor, value_grad


def whole(shape):
    return pl.BlockSpec(shape, lambda j: (0,) * len(shape))


def part(shape):
    return pl.BlockSpec((1,) + shape, lambda j: (j,) + (0,) * len(shape))


def shaped(shape, dtype=bf16):
    return jax.ShapeDtypeStruct(shape, dtype)


def by_piece(kernel, out_shape, in_specs, out_specs, scratch, args):
    return pl.pallas_call(
        kernel,
        out_shape=out_shape,
        grid=(4,),
        in_specs=in_specs,
        out_specs=out_specs,
        scratch_shapes=scratch,
        compiler_params=pltpu.CompilerParams(vmem_limit_bytes=48 * 2**20),
        cost_estimate=pl.CostEstimate(flops=0, bytes_accessed=0, transcendentals=0),
    )(*args)


def first_piece(action):
    pl.when(pl.program_id(0) == 0)(action)


def last_piece(action):
    pl.when(pl.program_id(0) == 3)(action)


def self_kernel(groups, x_ref, shift_ref, scale_ref, weight_ref, *refs):
    bias_ref = refs[0] if groups == 1 else None
    normed_ref, packed_ref, mixed_ref = refs[-3:]

    @first_piece
    def _():
        normed = norm_value(x_ref[...]) * (1.0 + scale_ref[...]) + shift_ref[...]
        normed_ref[...] = normed.astype(bf16)

    packed = product(normed_ref[...], weight_ref[0]).astype(bf16)
    packed_ref[0] = packed
    rows = 320 // groups
    for group in range(groups):
        mixed = []
        for head in range(2):
            queries, keys, values = (
                packed[group * rows : group * rows + rows, start : start + 72]
                for start in (72 * head, 144 + 72 * head, 288 + 72 * head)
            )
            bias = None if bias_ref is None else bias_ref[...]
            probability = softmax_value(queries, keys, bias).astype(bf16)
            mixed.append(product(probability, values))
        mixed_ref[0, group * rows : group * rows + rows, :] = jnp.concatenate(
            mixed, axis=1
        ).astype(bf16)


def self_forward(groups, hidden_state, shift, scale, weights, bias):
    specs = [whole((320, D)), whole((1, D)), whole((1, D)), part((D, 640))]
    args = [hidden_state, shift[None], scale[None], weights]
    if groups == 1:
        specs.append(whole((320, 320)))
        args.append(bias)
    return by_piece(
        partial(self_kernel, groups),
        [shaped((320, D)), shaped((4, 320, 640)), shaped((4, 320, 144))],
        specs,
        [whole((320, D)), part((320, 640)), part((320, 144))],
        [],
        args,
    )


def self_back_kernel(groups, extras, cuts, *refs):
    packed_ref, mixed_grad_ref, weight_ref, normed_ref = refs[:4]
    pairs = refs[4 : 4 + 2 * extras]
    bias_ref = refs[4 + 2 * extras] if groups == 1 else None
    normed_grad_ref, total_ref = refs[-2:]
    grad_refs = refs[-2 - len(cuts) : -2]
    packed, mixed_grad = packed_ref[0], mixed_grad_ref[0]
    rows = 320 // groups
    strips = []
    for group in range(groups):
        at = group * rows
        parts = []
        for head in range(2):
            queries, keys, values = (
                packed[at : at + rows, start : start + 72]
                for start in (72 * head, 144 + 72 * head, 288 + 72 * head)
            )
            bias = None if bias_ref is None else bias_ref[...]
            own_grad = mixed_grad[at : at + rows, 72 * head : 72 * head + 72]
            parts.append(head_back(queries, keys, values, own_grad, bias))
        line = [parts[head][which] for which in range(3) for head in range(2)]
        line.append(jnp.zeros((rows, 208), f32))
        strips.append(jnp.concatenate(line, axis=1).astype(bf16))
    packed_grad = strips[0] if groups == 1 else jnp.concatenate(strips, axis=0)
    width = weight_ref.shape[2]
    grad = outer_sum(normed_ref[...], packed_grad)
    if width > 640:
        grad = jnp.concatenate([grad, jnp.zeros((D, width - 640), f32)], axis=1)
    for n in range(extras):
        start = (384, 512, 640)[n]
        own = outer_sum(pairs[2 * n][...], pairs[2 * n + 1][0])
        lines = [grad[:, :start], grad[:, start : start + 256] + own, grad[:, start + 256 :]]
        grad = jnp.concatenate([line for line in lines if line.shape[1] > 0], axis=1)
    start = 0
    for cut, grad_ref in zip(cuts, grad_refs):
        grad_ref[0] = grad[:, start : start + cut].astype(bf16)
        start += cut
    back = product_back(packed_grad, weight_ref[0, :, :640])

    @first_piece
    def _():
        total_ref[...] = back

    @pl.when(pl.program_id(0) > 0)
    def _():
        total_ref[...] += back

    @last_piece
    def _():
        normed_grad_ref[...] = total_ref[...].astype(bf16)


def self_back(groups, packed, mixed_grad, weights, normed, pairs, bias, cuts):
    width = weights.shape[-1]
    specs = [part((320, 640)), part((320, 144)), part((D, width)), whole((320, D))]
    args = [packed, mixed_grad, weights, normed]
    for rows, window in pairs:
        specs += [whole((320, D)), part((320, 256))]
        args += [rows, window]
    if groups == 1:
        specs.append(whole((320, 320)))
        args.append(bias)
    results = by_piece(
        partial(self_back_kernel, groups, len(pairs), cuts),
        [shaped((4, D, cut)) for cut in cuts] + [shaped((320, D))],
        specs,
        [part((D, cut)) for cut in cuts] + [whole((320, D))],
        [pltpu.VMEM((320, D), f32)],
        args,
    )
    return results[:-1], results[-1]


def out_kernel(start, mixed_ref, weight_ref, out_ref):
    low = start // 128 * 128
    value = product(mixed_ref[...], weight_ref[0, :, low : low + 256])
    out_ref[0] = value[:, start - low : start - low + 144].astype(bf16)


def out_forward(mixed_rows, weights, start):
    return by_piece(
        partial(out_kernel, start),
        shaped((4, 320, 144)),
        [whole((320, D)), part(weights.shape[1:])],
        part((320, 144)),
        [],
        [mixed_rows, weights],
    )


def out_back_kernel(low, window_ref, weight_ref, out_ref, total_ref):
    back = product_back(window_ref[0], weight_ref[0, :, low : low + 256])

    @first_piece
    def _():
        total_ref[...] = back

    @pl.when(pl.program_id(0) > 0)
    def _():
        total_ref[...] += back

    @last_piece
    def _():
        for n in range(8):
            out_ref[n] = total_ref[:, 144 * n : 144 * n + 144].astype(bf16)


def out_back(window, weights, low):
    halves = by_piece(
        partial(out_back_kernel, low),
        shaped((8, 320, 144)),
        [part((320, 256)), part(weights.shape[1:])],
        whole((8, 320, 144)),
        [pltpu.VMEM((320, D), f32)],
        [window, weights],
    ).reshape(2, 4, 320, 144)
    core = lax.axis_index("c")
    keep = lax.dynamic_index_in_dim(halves, core, 0, keepdims=False)
    give = lax.dynamic_index_in_dim(halves, 1 - core, 0, keepdims=False)
    return (keep.astype(f32) + swap(give, "c").astype(f32)).astype(bf16)


def cross_kernel(x_ref, gain_ref, weight_ref, key_ref, value_ref, bias_ref, normed_ref, query_ref, mixed_ref):
    @first_piece
    def _():
        normed_ref[...] = (norm_value(x_ref[...]) * gain_ref[...]).astype(bf16)

    queries = product(normed_ref[...], weight_ref[0, :, 512:768]).astype(bf16)[:, 64:208]
    query_ref[0] = queries
    keys, values = key_ref[0], value_ref[0]
    mixed = []
    for head in range(2):
        own = slice(72 * head, 72 * head + 72)
        probability = softmax_value(queries[:, own], keys[:, own], bias_ref[...])
        mixed.append(product(probability.astype(bf16), values[:, own]))
    mixed_ref[0] = jnp.concatenate(mixed, axis=1).astype(bf16)


def cross_forward(hidden_state, gain, weights, keys, values, bias):
    return by_piece(
        cross_kernel,
        [shaped((320, D)), shaped((4, 320, 144)), shaped((4, 320, 144))],
        [whole((320, D)), whole((1, D)), part((D, 896))]
        + [part((128, 144)), part((128, 144)), whole((1, 128))],
        [whole((320, D)), part((320, 144)), part((320, 144))],
        [],
        [hidden_state, gain[None], weights, keys, values, bias],
    )


def cross_back_kernel(
    query_ref, key_ref, value_ref, grad_ref, weight_ref, bias_ref, window_ref, key_out, value_out, normed_ref, total_ref
):
    queries, keys, values, mixed_grad = query_ref[0], key_ref[0], value_ref[0], grad_ref[0]
    parts = []
    for head in range(2):
        own = slice(72 * head, 72 * head + 72)
        parts.append(
            head_back(queries[:, own], keys[:, own], values[:, own], mixed_grad[:, own], bias_ref[...])
        )
    zeros = jnp.zeros((320, 64), f32)
    window = jnp.concatenate(
        [zeros, parts[0][0], parts[1][0], zeros[:, :48]], axis=1
    ).astype(bf16)
    window_ref[0] = window
    key_out[0] = jnp.concatenate([parts[0][1], parts[1][1]], axis=1).astype(bf16)
    value_out[0] = jnp.concatenate([parts[0][2], parts[1][2]], axis=1).astype(bf16)
    back = product_back(window, weight_ref[0, :, 512:768])

    @first_piece
    def _():
        total_ref[...] = back

    @pl.when(pl.program_id(0) > 0)
    def _():
        total_ref[...] += back

    @last_piece
    def _():
        normed_ref[...] = total_ref[...].astype(bf16)


def cross_back(queries, keys, values, mixed_grad, weights, bias):
    return by_piece(
        cross_back_kernel,
        [shaped((4, 320, 256)), shaped((4, 128, 144)), shaped((4, 128, 144)), shaped((320, D))],
        [part((320, 144)), part((128, 144)), part((128, 144)), part((320, 144)), part((D, 896)), whole((1, 128))],
        [part((320, 256)), part((128, 144)), part((128, 144)), whole((320, D))],
        [pltpu.VMEM((320, D), f32)],
        [queries, keys, values, mixed_grad, weights, bias],
    )


GELU_SCALE = math.sqrt(2.0 / math.pi)


def down_halves(down_ref):
    blocks = [(y, 2 * z) for y in range(4) for z in range(2)]
    low = jnp.concatenate([down_ref[0, y, z] for y, z in blocks], axis=0)
    high = jnp.concatenate([down_ref[0, y, z + 1, :, :512] for y, z in blocks], axis=0)
    return low, high


def feed_kernel(x_ref, shift_ref, scale_ref, up_ref, down_ref, normed_ref, inner_ref, active_ref, out_ref, total_ref):
    @first_piece
    def _():
        normed = norm_value(x_ref[...]) * (1.0 + scale_ref[...]) + shift_ref[...]
        normed_ref[...] = normed.astype(bf16)

    inner = product(normed_ref[...], up_ref[0])
    inner_ref[0] = inner
    bent = jnp.tanh(GELU_SCALE * (inner + 0.044715 * inner * inner * inner))
    active = (0.5 * inner * (1.0 + bent)).astype(bf16)[:, :576]
    active_ref[0] = active
    low, high = down_halves(down_ref)

    @first_piece
    def _():
        total_ref[:, :640] = product(active, low)
        total_ref[:, 640:] = product(active, high)

    @pl.when(pl.program_id(0) > 0)
    def _():
        total_ref[:, :640] += product(active, low)
        total_ref[:, 640:] += product(active, high)

    @last_piece
    def _():
        out_ref[...] = total_ref[...].astype(bf16)


def feed_forward(hidden_state, shift, scale, up, down):
    return by_piece(
        feed_kernel,
        [shaped((320, D)), shaped((4, 320, 640), f32), shaped((4, 320, 576)), shaped((320, D))],
        [whole((320, D)), whole((1, D)), whole((1, D)), part((D, 640)), part((4, 4, 72, 640))],
        [whole((320, D)), part((320, 640)), part((320, 576)), whole((320, D))],
        [pltpu.VMEM((320, D), f32)],
        [hidden_state, shift[None], scale[None], up, down],
    )


def feed_back_kernel(
    grad_ref, inner_ref, active_ref, normed_ref, up_ref, down_ref, up_out, down_out, normed_grad_ref, total_ref
):
    low, high = down_halves(down_ref)
    low_grad, high_grad = grad_ref[:, :640], grad_ref[:, 640:]
    low_out = outer_sum(active_ref[0], low_grad).astype(bf16)
    high_out = outer_sum(active_ref[0], high_grad).astype(bf16)
    for block in range(8):
        rows = slice(72 * block, 72 * block + 72)
        down_out[0, block // 2, block % 2 * 2] = low_out[rows]
        down_out[0, block // 2, block % 2 * 2 + 1, :, :512] = high_out[rows]
        down_out[0, block // 2, block % 2 * 2 + 1, :, 512:] = jnp.zeros((72, 128), bf16)
    inner = inner_ref[0]
    active_grad = product_back(low_grad, low) + product_back(high_grad, high)
    active_grad = jnp.concatenate([active_grad, jnp.zeros((320, 64), f32)], axis=1)
    square = inner * inner
    bent = jnp.tanh(GELU_SCALE * inner * (1.0 + 0.044715 * square))
    slope = 0.5 * (1.0 + bent) + 0.5 * inner * (1.0 - bent * bent) * GELU_SCALE * (
        1.0 + 0.134145 * square
    )
    inner_grad = (active_grad * slope).astype(bf16)
    up_out[0] = outer_sum(normed_ref[...], inner_grad).astype(bf16)
    back = product_back(inner_grad, up_ref[0])

    @first_piece
    def _():
        total_ref[...] = back

    @pl.when(pl.program_id(0) > 0)
    def _():
        total_ref[...] += back

    @last_piece
    def _():
        normed_grad_ref[...] = total_ref[...].astype(bf16)


def feed_back(output_grad, inner, active, normed, up, down):
    return by_piece(
        feed_back_kernel,
        [shaped((4, D, 640)), shaped((4, 4, 4, 72, 640)), shaped((320, D))],
        [whole((320, D)), part((320, 640)), part((320, 576)), whole((320, D))]
        + [part((D, 640)), part((4, 4, 72, 640))],
        [part((D, 640)), part((4, 4, 72, 640)), whole((320, D))],
        [pltpu.VMEM((320, D), f32)],
        [output_grad, inner, active, normed, up, down],
    )


def words_kernel(text_ref, grad_ref, out_ref):
    out_ref[...] = outer_sum(text_ref[...], grad_ref[...]).astype(bf16)


def words_back(text, grad):
    return pl.pallas_call(
        words_kernel,
        out_shape=shaped((4096, 640)),
        grid=(8,),
        in_specs=[
            pl.BlockSpec((120, 512), lambda j: (0, j)),
            pl.BlockSpec((120, 640), lambda j: (0, 0)),
        ],
        out_specs=pl.BlockSpec((512, 640), lambda j: (j, 0)),
        compiler_params=pltpu.CompilerParams(vmem_limit_bytes=40 * 2**20),
        cost_estimate=pl.CostEstimate(flops=0, bytes_accessed=0, transcendentals=0),
    )(text, grad)


def both_cores(partial_rows):
    return partial_rows.astype(f32) + swap(partial_rows, "c").astype(f32)


def attention_block(groups, hidden_state, modulation, weights, bias):
    normed, packed, mixed = self_forward(
        groups, hidden_state, modulation[0], modulation[1], weights, bias
    )
    mixed_rows = apart(mixed)
    branch = apart(out_forward(mixed_rows, weights, 432)).astype(f32)
    stored = (hidden_state, normed, packed, mixed_rows, branch)
    return (hidden_state + modulation[2] * branch, stored)


def attention_block_back(groups, incoming, stored, modulation, weights, pairs, bias, earlier, cuts):
    hidden_state, normed, packed, mixed_rows, branch = stored
    gate_grad = jnp.sum(incoming * branch, axis=0)
    branch_grad = (modulation[2] * incoming).astype(bf16)
    window = windows(own_columns(branch_grad), 48)
    mixed_grad = after(out_back(window, weights, 384), earlier)
    weight_grad, normed_grad = self_back(
        groups, packed, mixed_grad, weights, normed, [(mixed_rows, window)] + pairs, bias, cuts
    )
    normed_grad = both_cores(normed_grad)
    normal_rows, inverse_std = normalize(hidden_state)
    scale_grad = jnp.sum(normed_grad * normal_rows, axis=0)
    shift_grad = jnp.sum(normed_grad, axis=0)
    upstream = incoming + norm_back(normal_rows, inverse_std, normed_grad * (1.0 + modulation[1]))
    return (upstream, weight_grad, (shift_grad, scale_grad, gate_grad))


def feed_block(hidden_state, modulation, up, down):
    normed, inner, active, output = feed_forward(
        hidden_state, modulation[3], modulation[4], up, down
    )
    output = both_cores(output)
    return (hidden_state + modulation[5] * output, (hidden_state, normed, inner, active, output))


def feed_block_back(incoming, stored, modulation, up, down):
    hidden_state, normed, inner, active, output = stored
    gate_grad = jnp.sum(incoming * output, axis=0)
    output_grad = (modulation[5] * incoming).astype(bf16)
    up_grad, down_grad, normed_grad = feed_back(output_grad, inner, active, normed, up, down)
    normed_grad = both_cores(normed_grad)
    normal_rows, inverse_std = normalize(hidden_state)
    scale_grad = jnp.sum(normed_grad * normal_rows, axis=0)
    shift_grad = jnp.sum(normed_grad, axis=0)
    upstream = incoming + norm_back(normal_rows, inverse_std, normed_grad * (1.0 + modulation[4]))
    return (upstream, up_grad, down_grad, (shift_grad, scale_grad, gate_grad))


def scatter_ring(grad):
    return lax.psum_scatter(grad, RING, scatter_dimension=0, tiled=False)


def own_columns(value):
    half = value.shape[1] // 2
    return jnp.where(lax.axis_index("c") == 0, value[:, :half], value[:, half:])


def local(
    latents,
    noise_sample,
    timesteps,
    text_states,
    text_lengths,
    cotangent,
    time_input,
    time_output,
    spatial_table,
    spatial_projection,
    spatial_output,
    spatial_up,
    spatial_down,
    temporal_table,
    temporal_projection,
    temporal_output,
    cross_query,
    cross_text,
    cross_output,
    cross_gain,
    temporal_up,
    temporal_down,
):
    core, far = lax.axis_index("c"), lax.axis_index("xh")
    clip = (lax.axis_index("y") * 4 + lax.axis_index("z")) * 2 + lax.axis_index("xl")
    me = clip * 4 + far * 2 + core

    sent = jnp.concatenate(
        [
            to_pieces(spatial_up, 1),
            to_pieces(spatial_projection, 3),
            to_pieces(spatial_output, 1),
            to_pieces(temporal_up, 1),
            to_pieces(temporal_projection, 3),
            to_pieces(temporal_output, 1),
            to_pieces(cross_query, 1),
            to_pieces(cross_output, 1),
        ],
        axis=2,
    )
    words = cross_text.reshape(4, 8, 2, 2, 2, 288).transpose(4, 3, 1, 0, 2, 5).reshape(4, 8, 2304)
    words = jnp.pad(words, ((0, 0), (0, 1), (0, 0)))
    near = lax.axis_index("xl")
    words = jnp.stack([jnp.where(near == 0, words, 0), jnp.where(near == 1, words, 0)])
    split_steps = jnp.stack([timesteps // 32, timesteps % 32], axis=1).reshape(-1).astype(bf16)
    note = [spatial_table.reshape(-1), temporal_table.reshape(-1), cross_gain, split_steps]
    note = jnp.pad(jnp.concatenate(note), (0, 9))[None]
    note = jnp.concatenate([time_input.reshape(9, 256), jnp.pad(note, ((0, 8), (0, 0)))], axis=1)
    note = jnp.broadcast_to(note, (8, 9, 384))
    sent = jnp.concatenate([sent, words.reshape(8, 9, 2304), note], axis=2)
    mine = swap_group(sent, GROUP)
    note = mine[..., 4896:].reshape(72, 384)
    words = lax.dynamic_slice_in_dim(mine[:, :8, 2592:4896], near * 4, 4, 0)
    words = words.reshape(4, 8, 4, 576).transpose(0, 2, 1, 3).reshape(128, 576)
    words = widen(words, 640)
    mine = mine[..., :2592].reshape(72, 2592)
    shards = jnp.stack([spatial_down, temporal_down])
    s_up = widen(mine[:, :576], 640)
    s_att = widen(mine[:, 576:1152], 640)
    t_up = widen(mine[:, 1152:1728], 640)
    t_att = widen(mine[:, 1728:2592], 896)
    downs = send_down(shards)

    near_words = by_core(words, swap(words, "xl"), "xl", 0)
    rings, first_done = fetch_rings(
        [
            (jnp.concatenate([t_up, s_att, downs[1], note], axis=1), "y"),
            (jnp.concatenate([s_up, t_att, downs[0]], axis=1), "z"),
        ],
        (),
    )
    t_up, att_down, note = place(rings[0], "y", 0, (640, 1280, 384))
    up_att, s_down = place(rings[1], "z", 0, (1536, 640))
    across = lax.all_gather(
        jnp.concatenate([att_down, s_down], axis=2), RING, axis=0, tiled=False
    )
    s_att, t_down, s_down = across[..., :640], across[..., 640:1280], across[..., 1280:]
    up_words = jnp.concatenate([t_up, near_words.reshape(4, 64, 640), widen(note, 640)], axis=1)
    rings, second_done = gather_rings([(up_att, "y"), (up_words, "z")], first_done)
    s_up, t_att = place(rings[0], "y", 0, (640, 896))
    (up_words,) = place(rings[1], "z", 1, (640,))
    t_up, words = up_words[:, :, :72], jnp.swapaxes(up_words[:, :, 72:136], 0, 1)
    notes = up_words[:, :, 136:, :384].reshape(16, 8, 9, 384)
    full_time_input = notes[..., :256].reshape(FREQ, D)
    notes = notes[:, :, 0, 256:].reshape(128, 128)
    steps = notes[::4, 117:119].astype(f32)
    steps = (steps[:, 0] * 32.0 + steps[:, 1]).astype(jnp.int32)
    embedded = time_features(steps, FREQ).astype(bf16)
    pre_time = product(embedded, full_time_input)
    lifted = jax.nn.silu(pre_time).astype(bf16)
    own_lifted = lax.dynamic_slice_in_dim(lifted, me * 9, 9, 1)
    shares = product(own_lifted, time_output)
    shares = swap_group(shares.reshape(128, 1728), ALL)
    s_up = lax.all_gather(s_up.reshape(D, 640), RING, axis=0, tiled=False)
    t_att = lax.all_gather(t_att.reshape(D, 896), RING, axis=0, tiled=False)
    words = lax.all_gather(words.reshape(1024, 640), "y", axis=0, tiled=False).reshape(4096, 640)
    t_up = lax.all_gather(t_up.reshape(D, 640), RING, axis=0, tiled=False)

    tables = notes[:, :108].reshape(128, 12, 9).transpose(1, 0, 2).reshape(2, 6, D)
    full_gain = notes[:, 108:117].reshape(D).astype(f32)
    shared = jnp.sum(shares, axis=0)
    shared = by_core(shared, swap(shared, "c"), "c", 0)
    shared = by_core(shared, swap(shared, "xh"), "xh", 0).reshape(6, D)
    rings, third_done = gather_rings([(s_att, "z"), (s_down, "y")], second_done)
    (s_att,) = place(rings[0], "z", 2, (640,))
    s_att = s_att.reshape(4, D, 640)
    (s_down,) = place(rings[1], "y", 1, (640,))
    rings, _ = gather_rings([(t_down, "z")], third_done)
    (t_down,) = place(rings[0], "z", 2, (640,))

    spatial_mod = tables[0].astype(f32) + shared
    temporal_mod = tables[1].astype(f32) + shared

    alpha_bars = noise_table(STEPS)
    picked = jnp.sum(jnp.where(jnp.arange(STEPS) == timesteps[0], alpha_bars, 0.0))
    signal_scale = jnp.sqrt(picked)

    frames = jnp.stack([latents[0, 0], noise_sample[0, 0]])
    other = swap(frames, "c")

    def noised(pair):
        return signal_scale * pair[0].astype(f32) + jnp.sqrt(1.0 - picked) * pair[1].astype(f32)

    hidden_state = by_core(noised(frames), noised(other), "c", 0)

    hidden_state, spatial_attention = attention_block(2, hidden_state, spatial_mod, s_att, None)
    hidden_state, spatial_mlp = feed_block(hidden_state, spatial_mod, s_up, s_down)

    def to_patches(rows):
        halves = rows.reshape(2, 2, 80, D)
        keep = lax.dynamic_index_in_dim(halves, far, 1, keepdims=False)
        give = lax.dynamic_index_in_dim(halves, 1 - far, 1, keepdims=False)
        return jnp.concatenate([keep, swap(give, "xh")], axis=0).reshape(320, D)

    patch_rows = to_patches(hidden_state.astype(bf16))
    own_cotangent = cotangent[0, 0]
    incoming = to_patches(by_core(own_cotangent, swap(own_cotangent, "c"), "c", 0)).astype(f32)

    text_order = text_states[0]
    text_rows = product(text_order, words)[:, :576].astype(bf16)
    other_text = swap(text_rows, "xh")
    def text_pieces(value):
        pieces = jnp.swapaxes(value.reshape(120, 4, 144), 0, 1)
        return jnp.pad(pieces, ((0, 0), (0, 8), (0, 0)))

    text_keys = text_pieces(by_core(text_rows[:, :288], other_text[:, :288], "xh", 1))
    text_values = text_pieces(by_core(text_rows[:, 288:], other_text[:, 288:], "xh", 1))
    text_bias = jnp.where(jnp.arange(128) < text_lengths[0], 0.0, MASK_FILL)[None]
    row = jnp.arange(320) % 80
    patch_bias = jnp.where(row[:, None] == row[None], 0.0, MASK_FILL)

    hidden_state = patch_rows.astype(f32)
    hidden_state, temporal_attention = attention_block(
        1, hidden_state, temporal_mod, t_att, patch_bias
    )
    cross_state = hidden_state
    cross_normed, cross_queries, cross_mixed = cross_forward(
        cross_state, full_gain, t_att, text_keys, text_values, text_bias
    )
    cross_mixed = apart(cross_mixed)
    hidden_state = cross_state + apart(out_forward(cross_mixed, t_att, 720)).astype(f32)
    hidden_state, temporal_mlp = feed_block(hidden_state, temporal_mod, t_up, t_down)

    finished = hidden_state.astype(bf16).reshape(4, 80, D)
    keep = lax.dynamic_index_in_dim(finished, core, 0, keepdims=False)
    give = lax.dynamic_index_in_dim(finished, 2 + core, 0, keepdims=False)
    activations = by_core(keep, swap(give, "xh"), "xh", 0)[None, None]

    incoming, t_up_grad, t_down_grad, t_mlp_mod = feed_block_back(
        incoming, temporal_mlp, temporal_mod, t_up, t_down
    )
    t_up_grad = scatter_ring(t_up_grad)
    t_down_grad = scatter_ring(t_down_grad.reshape(4, D, 640))
    cross_grad = incoming.astype(bf16)
    out_window = windows(own_columns(cross_grad), 80)
    cross_mixed_grad = out_back(out_window, t_att, 640)
    query_window, key_grad, value_grad, normed_grad = cross_back(
        cross_queries, text_keys, text_values, cross_mixed_grad, t_att, text_bias
    )
    normed_grad = both_cores(normed_grad)
    normal_rows, inverse_std = normalize(cross_state)
    gain_grad = jnp.sum(normed_grad * normal_rows, axis=0)
    incoming = incoming + norm_back(normal_rows, inverse_std, normed_grad * full_gain)
    key_grad = jnp.swapaxes(key_grad[:, :120], 0, 1).reshape(120, 576)
    value_grad = jnp.swapaxes(value_grad[:, :120], 0, 1).reshape(120, 576)

    def text_half(which):
        def half(value):
            return lax.dynamic_slice_in_dim(value, which * 288, 288, 1)

        return jnp.concatenate([half(key_grad), half(value_grad)], axis=1)

    text_grad = text_half(far).astype(f32) + swap(text_half(1 - far), "xh").astype(f32)
    words_grad = words_back(text_order, widen(text_grad.astype(bf16), 640))
    incoming, t_att_grad, t_att_mod = attention_block_back(
        1,
        incoming,
        temporal_attention,
        temporal_mod,
        t_att,
        [(cross_normed, query_window), (cross_mixed, out_window)],
        patch_bias,
        (text_grad, t_up_grad),
        (896,),
    )
    t_mod_grad = jnp.stack(t_att_mod + t_mlp_mod)

    back = incoming.astype(bf16).reshape(4, 80, D)
    theirs = swap(back[2:], "xh")
    t_att_grad = scatter_ring(tie(t_att_grad[0], t_down_grad))


    frame_grad = by_core(back[:2], theirs, "xh", 1).reshape(320, D).astype(f32)
    words_grad = tie(words_grad, t_att_grad).reshape(4, 1024, 640)
    words_grad = lax.psum_scatter(words_grad, "y", scatter_dimension=0, tiled=False)
    words_grad = words_grad.reshape(4, 256, 640)
    words_grad = lax.psum_scatter(words_grad, "z", scatter_dimension=0, tiled=False)
    words_grad = words_grad.reshape(2, 128, 640)
    words_grad = lax.dynamic_index_in_dim(words_grad, near, 0, keepdims=False).astype(f32) + swap(
        lax.dynamic_index_in_dim(words_grad, 1 - near, 0, keepdims=False), "xl"
    ).astype(f32)
    words_grad = words_grad.astype(bf16)
    frame_grad, s_up_grad, s_down_grad, s_mlp_mod = feed_block_back(
        frame_grad, spatial_mlp, spatial_mod, s_up, s_down
    )
    s_up_grad = s_up_grad.reshape(4, 4, 4, 72, 640)
    (s_up_grad, s_down_grad), s_done, _ = scatter_rings(
        [([(s_up_grad, 2)], "z"), ([(s_down_grad, 1)], "y")], ()
    )
    frame_grad, s_att_grad, s_att_mod = attention_block_back(
        2, frame_grad, spatial_attention, spatial_mod, s_att, [], None, (s_done, t_down_grad), (384, 256)
    )
    t_up_grad = tie(t_up_grad, s_att_grad[0])
    t_grads = jnp.concatenate([t_up_grad, t_att_grad, t_down_grad], axis=1)
    t_grads = t_grads.reshape(4, 288, 2176)
    t_grads = lax.psum_scatter(t_grads, "y", scatter_dimension=0, tiled=False)
    t_grads = t_grads.reshape(4, 72, 2176)
    t_grads = lax.psum_scatter(t_grads, "z", scatter_dimension=0, tiled=False)
    latent_grad = signal_scale * lax.dynamic_index_in_dim(frame_grad.reshape(2, 160, D), core, 0)
    s_mod_grad = jnp.stack(s_att_mod + s_mlp_mod)
    s_att_grad = [grad.reshape(4, 4, 4, 72, -1) for grad in s_att_grad]
    (att_x_y, att_x_z), _, done = scatter_rings(
        [([(s_att_grad[0], 2)], "z"), ([(s_att_grad[1], 1)], "y")], ()
    )
    (up, down), done = sum_rings(
        [([(s_up_grad, 1), (att_x_y, 1)], "y"), ([(s_down_grad, 0), (att_x_z, 0)], "x")], done
    )
    (up, down), done = sum_rings([([(up, 0)], "x"), ([(down, 0)], "z")], done)
    downs = return_down(jnp.stack([down[:, :640], t_grads[:, 1536:]])).astype(f32)
    s_down_done, t_down_done = downs[0], downs[1]
    words_grad = swap_group(words_grad[:, :576].reshape(4, 32, 576), SEQ)
    words_grad = words_grad.reshape(2, 2, 32, 2, 288).transpose(2, 3, 1, 0, 4).reshape(32, 2304)

    returned = jnp.concatenate(
        [
            up[:, :576],
            up[:, 640:],
            down[:, 640:832],
            t_grads[:, :576],
            t_grads[:, 640:1504],
        ],
        axis=1,
    )
    returned = swap_group(returned.reshape(8, 9, 2592), GROUP).astype(f32)
    s_up_grad = from_pieces(returned[..., :576], 1)
    s_proj_grad = from_pieces(returned[..., 576:1008], 3)
    s_out_grad = from_pieces(returned[..., 1008:1152], 1)
    t_up_grad = from_pieces(returned[..., 1152:1728], 1)
    t_proj_grad = from_pieces(returned[..., 1728:2160], 3)
    t_out_grad = from_pieces(returned[..., 2160:2304], 1)
    x_query_grad = from_pieces(returned[..., 2304:2448], 1)
    x_out_grad = from_pieces(returned[..., 2448:], 1)

    shared_grad = (s_mod_grad + t_mod_grad).reshape(4, 1728)
    shared_grad = shared_grad + swap(shared_grad, "xh")
    quarter = lax.dynamic_index_in_dim(shared_grad, far * 2 + core, 0, keepdims=False)
    table_part = jnp.stack([s_mod_grad, t_mod_grad]).reshape(12, 128, 9).transpose(1, 0, 2)
    table_part = jnp.concatenate([table_part.reshape(128, 108), gain_grad.reshape(128, 9)], axis=1)
    table_part = jnp.where(core == 0, table_part, 0.0)
    letter = jnp.concatenate(
        [jnp.broadcast_to(quarter, (128, 1728)), table_part, jnp.zeros((128, 75), f32)], axis=1
    )
    letters = swap_group(letter, ALL)
    all_shared = letters[:, :1728].reshape(32, 6 * D)
    table_sum = jnp.sum(letters[:, 1728:1845], axis=0)
    s_table_grad = table_sum[:54].reshape(6, 9)
    t_table_grad = table_sum[54:108].reshape(6, 9)
    cross_gain_grad = table_sum[108:]

    def exact(a, b, dims):
        return lax.dot_general(
            a, b, (dims, ((), ())), precision=lax.Precision.HIGHEST, preferred_element_type=f32
        )

    time_output_grad = exact(own_lifted.astype(f32), all_shared, ((0,), (0,)))
    lifted_grad = exact(all_shared, time_output.astype(f32), ((1,), (1,)))
    own_pre = lax.dynamic_slice_in_dim(pre_time, me * 9, 9, 1)
    own_pre_grad = jax.vjp(jax.nn.silu, own_pre)[1](lifted_grad)[0]
    card = jnp.broadcast_to(widen(own_pre_grad.reshape(288), 384), (128, 384))
    cards = swap_group(card, ALL)[:, :288].reshape(128, 32, 9)
    pre_grad = cards.transpose(1, 0, 2).reshape(32, D)
    own_embedded = lax.dynamic_slice_in_dim(embedded, me * 2, 2, 1).astype(f32)
    time_input_grad = exact(own_embedded, pre_grad, ((0,), (0,)))

    return (
        activations,
        latent_grad[None],
        time_input_grad,
        time_output_grad,
        s_table_grad,
        s_proj_grad,
        s_out_grad,
        s_up_grad,
        s_down_done,
        t_table_grad,
        t_proj_grad,
        t_out_grad,
        x_query_grad,
        words_grad.astype(f32),
        x_out_grad,
        cross_gain_grad,
        t_up_grad,
        t_down_done,
    )


def solution(mesh):
    fine = Mesh(mesh.devices.reshape(4, 4, 2, 2, 2), ALL)
    frames = P(CLIP, SEQ, None, None)
    rows = P(ALL, None)
    columns = P(None, ALL)
    in_specs = (
        frames,
        frames,
        P(CLIP),
        P(CLIP, None, None),
        P(CLIP),
        frames,
        rows,
        rows,
        columns,
        rows,
        rows,
        rows,
        rows,
        columns,
        rows,
        rows,
        rows,
        rows,
        rows,
        P(ALL),
        rows,
        rows,
    )
    out_specs = (
        frames,
        frames,
        rows,
        rows,
        columns,
        rows,
        rows,
        rows,
        rows,
        columns,
        rows,
        rows,
        rows,
        rows,
        rows,
        P(ALL),
        rows,
        rows,
    )
    return jax.shard_map(local, mesh=fine, in_specs=in_specs, out_specs=out_specs, check_vma=False)
```

```python
from functools import partial
import math

import jax
import jax.numpy as jnp
from jax import lax
from jax.experimental import pallas as pl
from jax.experimental.pallas import tpu as pltpu
from jax.sharding import Mesh, PartitionSpec as P

HEADS = 16
HEAD_DIM = 72
FREQ = 256
STEPS = 1000
D = 1152
FFN = 4608
EPSILON = 1e-06
MASK_FILL = -1000000000.0

CLIP = ("y", "z", "xl")
SEQ = ("xh", "c")
GROUP = ("xl", "xh", "c")
RING = ("xh", "xl")
ALL = ("y", "z", "xl", "xh", "c")
X_PLACE = (0, 2, 1, 3)

bf16 = jnp.bfloat16
f32 = jnp.float32


def fetch(value, axis, step):
    if axis == "x":
        pairs = [(X_PLACE[(i + step) % 4], X_PLACE[i]) for i in range(4)]
        return lax.ppermute(value, ("xl", "xh"), pairs)
    return lax.ppermute(value, axis, [((i + step) % 4, i) for i in range(4)])


def swap(value, axis):
    return lax.ppermute(value, axis, [(0, 1), (1, 0)])


def place_of(axis):
    if axis == "x":
        return lax.axis_index("xh") * 2 + lax.axis_index("xl")
    return lax.axis_index(axis)


def turn(step, row, which, rows):
    return jnp.where(step == which, row, jnp.where(step < which, 0, rows - 1))


def place_kernel(widths, own_ref, *refs):
    blocks, outs = refs[:4], refs[4:]
    for which in range(4):

        @pl.when(pl.program_id(0) == which)
        def _():
            start = 0
            for width, out in zip(widths, outs):
                out[...] = blocks[which][..., start : start + width].reshape(out.shape)
                start += width


def place(blocks, axis, pos, widths):
    lead, last = blocks[0].shape[:pos], blocks[0].shape[pos:]
    rows = math.prod(lead)
    group = min(rows, 4)
    rows //= group
    flat = [block.reshape((rows, group) + last) for block in blocks]
    zeros = (0,) * len(last)
    whole = (group,) + last

    def in_map(which):
        return lambda step, row, own: (turn(step, row, which, rows), 0) + zeros

    def out_map(step, row, own):
        return (row, 0, lax.rem(own[0] + step, 4)) + zeros

    outs = pl.pallas_call(
        partial(place_kernel, widths),
        out_shape=[
            jax.ShapeDtypeStruct((rows, group, 4) + last[:-1] + (width,), bf16) for width in widths
        ],
        grid_spec=pltpu.PrefetchScalarGridSpec(
            num_scalar_prefetch=1,
            grid=(4, rows),
            in_specs=[pl.BlockSpec((1,) + whole, in_map(which)) for which in range(4)],
            out_specs=[
                pl.BlockSpec((1, group, 1) + last[:-1] + (width,), out_map) for width in widths
            ],
        ),
        compiler_params=pltpu.CompilerParams(vmem_limit_bytes=40 * 2**20),
        cost_estimate=pl.CostEstimate(flops=0, bytes_accessed=0, transcendentals=0),
    )(place_of(axis).reshape(1), *flat)
    return [out.reshape(lead + out.shape[2:]) for out in outs]


def ring_blocks(value, axis):
    return [value] + [fetch(value, axis, step) for step in (1, 3, 2)]


def in_order(blocks):
    return [blocks[0], blocks[1], blocks[3], blocks[2]]


def after(values, earlier):
    return lax.optimization_barrier((values, earlier))[0]


def tie_kernel(*refs):
    pass


def tie(value, *earlier):
    anywhere = pl.BlockSpec(memory_space=pl.ANY)
    return pl.pallas_call(
        tie_kernel,
        out_shape=jax.ShapeDtypeStruct(value.shape, value.dtype),
        in_specs=[anywhere] * (1 + len(earlier)),
        out_specs=anywhere,
        input_output_aliases={0: 0},
        cost_estimate=pl.CostEstimate(flops=0, bytes_accessed=0, transcendentals=0),
    )(value, *earlier)


def fetch_rings(jobs, earlier):
    values = after([value for value, _ in jobs], earlier)
    blocks = [[value] for value, _ in jobs]
    for step in (1, 3, 2):
        for n, (_, axis) in enumerate(jobs):
            blocks[n].append(fetch(values[n], axis, step))
    blocks = lax.optimization_barrier(blocks)
    return [in_order(own) for own in blocks], [own[1] for own in blocks]


def gather_rings(jobs, earlier):
    values = after([value for value, _ in jobs], earlier)
    near = [(fetch(v, axis, 1), fetch(v, axis, 3)) for v, (_, axis) in zip(values, jobs)]
    near = lax.optimization_barrier(near)
    half = [value.shape[0] // 2 for value in values]
    across = [
        (fetch(up[:h], axis, 1), fetch(down[h:], axis, 3))
        for (up, down), h, (_, axis) in zip(near, half, jobs)
    ]
    near, across = lax.optimization_barrier((near, across))
    blocks = [
        [value, up, jnp.concatenate(pair, axis=0), down]
        for (value, _), (up, down), pair in zip(jobs, near, across)
    ]
    return blocks, [pair[0] for pair in across]


def ring_block(parts, axis, step):
    blocks = [pick(value, axis, step, pos) for value, pos in parts]
    return blocks[0] if len(blocks) == 1 else jnp.concatenate(blocks, axis=-1)


def add(*values):
    total = values[0].astype(f32)
    for value in values[1:]:
        total = total + value.astype(f32)
    return total.astype(bf16)


def sum_rings(jobs, earlier):
    sent = [[ring_block(parts, axis, step) for step in (1, 3, 2)] for parts, axis in jobs]
    sent = after(sent, earlier)
    arrived = [
        [fetch(own[k], axis, 4 - step) for k, step in enumerate((1, 3, 2))]
        for own, (_, axis) in zip(sent, jobs)
    ]
    arrived = lax.optimization_barrier(arrived)
    totals = [add(ring_block(parts, axis, 0), *own) for own, (parts, axis) in zip(arrived, jobs)]
    return totals, [own[0] for own in arrived]


def scatter_rings(jobs, earlier):
    sent = after([ring_block(parts, axis, 2) for parts, axis in jobs], earlier)
    half = [value.shape[0] // 2 for value in sent]
    across = [
        (fetch(value[:h], axis, 3), fetch(value[h:], axis, 1))
        for value, h, (_, axis) in zip(sent, half, jobs)
    ]
    across = lax.optimization_barrier(across)
    near = []
    for (low, high), h, (parts, axis) in zip(across, half, jobs):
        up, down = ring_block(parts, axis, 1), ring_block(parts, axis, 3)
        up = jnp.concatenate([add(up[:h], low), up[h:]], axis=0)
        down = jnp.concatenate([down[:h], add(down[h:], high)], axis=0)
        near.append((up, down))
    near = lax.optimization_barrier(near)
    near = [
        (fetch(up, axis, 3), fetch(down, axis, 1)) for (up, down), (_, axis) in zip(near, jobs)
    ]
    near = lax.optimization_barrier(near)
    totals = [add(ring_block(parts, axis, 0), *pair) for pair, (parts, axis) in zip(near, jobs)]
    return totals, [pair[0] for pair in across], [pair[0] for pair in near]


def pick(value, axis, step, pos):
    return lax.dynamic_index_in_dim(
        value, lax.rem(place_of(axis) + step, 4), pos, keepdims=False
    )


def by_core(first, second, axis, dim):
    own_first = lax.axis_index(axis) == 0
    return jnp.concatenate(
        [jnp.where(own_first, first, second), jnp.where(own_first, second, first)], axis=dim
    )


def down_pairs(other):
    pairs = []
    for d in range(128):
        y1, y0, z1, z0 = (d >> 6) & 1, (d >> 5) & 1, (d >> 4) & 1, (d >> 3) & 1
        xl, xh, core = (d >> 2) & 1, (d >> 1) & 1, d & 1
        half = 1 - core if other else core
        target = 0
        for bit in (z0, xl, xh, half, z1, y0, y1):
            target = 2 * target + bit
        pairs.append((d, target))
    return pairs


def send_down(shards):
    core = lax.axis_index("c")
    low = shards[:, :, :640]
    high = jnp.pad(shards[:, :, 640:], ((0, 0), (0, 0), (0, 128)))
    first = lax.ppermute(jnp.where(core == 0, low, high), ALL, down_pairs(False))
    second = lax.ppermute(jnp.where(core == 0, high, low), ALL, down_pairs(True))
    half = lax.axis_index("z") % 2
    return jnp.concatenate(
        [jnp.where(half == 0, first, second), jnp.where(half == 0, second, first)], axis=1
    )


def return_down(blocks):
    half = lax.axis_index("z") % 2
    top, bottom = blocks[:, :36], blocks[:, 36:]
    back = [[(b, a) for a, b in down_pairs(other)] for other in (False, True)]
    first = lax.ppermute(jnp.where(half == 0, top, bottom), ALL, back[0])
    second = lax.ppermute(jnp.where(half == 0, bottom, top), ALL, back[1])
    core = lax.axis_index("c")
    low = jnp.where(core == 0, first, second)
    high = jnp.where(core == 0, second, first)
    return jnp.concatenate([low, high[:, :, :512]], axis=2)


def to_pieces(shard, groups):
    rows = shard.shape[0]
    value = shard.reshape(rows, groups, 2, 2, 2, -1)
    value = value.transpose(4, 3, 2, 0, 1, 5)
    return value.reshape(8, rows, -1)


def from_pieces(value, groups):
    rows = value.shape[1]
    value = value.reshape(2, 2, 2, rows, groups, -1)
    value = value.transpose(3, 4, 2, 1, 0, 5)
    return value.reshape(rows, -1)


def swap_group(value, axes):
    return lax.all_to_all(value, axes, split_axis=0, concat_axis=0, tiled=True)


def widen(value, width):
    return jnp.pad(value, [(0, 0)] * (value.ndim - 1) + [(0, width - value.shape[-1])])


def noise_table(count):
    beta_values = jnp.linspace(0.0001, 0.02, count, dtype=f32)
    return jnp.cumprod(1.0 - beta_values)


def time_features(timesteps, feature_count):
    half_count = feature_count // 2
    frequency = jnp.exp(-math.log(10000.0) * jnp.arange(half_count, dtype=f32) / half_count)
    angles = timesteps.astype(f32)[:, None] * frequency
    return jnp.concatenate([jnp.cos(angles), jnp.sin(angles)], axis=1)


def normalize(values):
    average = jnp.mean(values, axis=-1, keepdims=True)
    centred = values - average
    inverse_std = lax.rsqrt(jnp.mean(centred * centred, axis=-1, keepdims=True) + EPSILON)
    return (centred * inverse_std, inverse_std)


def norm_back(normal_rows, inverse_std, normal_grad):
    first_mean = jnp.mean(normal_grad, axis=-1, keepdims=True)
    second_mean = jnp.mean(normal_grad * normal_rows, axis=-1, keepdims=True)
    return inverse_std * (normal_grad - first_mean - normal_rows * second_mean)


def product(operand, weight):
    return jnp.dot(operand, weight, preferred_element_type=f32)


def product_back(operand, weight):
    return lax.dot_general(operand, weight, (((1,), (1,)), ((), ())), preferred_element_type=f32)


def outer_sum(operand, partner):
    return lax.dot_general(operand, partner, (((0,), (0,)), ((), ())), preferred_element_type=f32)


def apart(own):
    other = swap(own, "c")
    first = lax.axis_index("c") == 0
    low, high = jnp.where(first, own, other), jnp.where(first, other, own)
    return jnp.concatenate([low[j] for j in range(4)] + [high[j] for j in range(4)], axis=1)


def windows(value, start):
    rows = value.shape[0]
    pieces = jnp.swapaxes(value.reshape(rows, 4, 144), 0, 1)
    return jnp.pad(pieces, ((0, 0), (0, 0), (start, 112 - start)))


def norm_value(values):
    centred = values - jnp.mean(values, axis=-1, keepdims=True)
    return centred * lax.rsqrt(jnp.mean(centred * centred, axis=-1, keepdims=True) + EPSILON)


def softmax_value(queries, keys, bias):
    scores = product_back(queries, keys) * HEAD_DIM ** (-0.5)
    if bias is not None:
        scores = scores + bias
    exponent = jnp.exp(scores - jnp.max(scores, axis=-1, keepdims=True))
    return exponent / jnp.sum(exponent, axis=-1, keepdims=True)


def head_back(queries, keys, values, mixed_grad, bias):
    factor = HEAD_DIM ** (-0.5)
    probability = softmax_value(queries, keys, bias)
    prob_grad = product_back(mixed_grad, values)
    value_grad = outer_sum(probability.astype(bf16), mixed_grad)
    inner = jnp.sum(probability * prob_grad, axis=-1, keepdims=True)
    score_grad = (probability * (prob_grad - inner)).astype(bf16)
    return product(score_grad, keys) * factor, outer_sum(score_grad, queries) * factor, value_grad


def whole(shape):
    return pl.BlockSpec(shape, lambda j: (0,) * len(shape))


def part(shape):
    return pl.BlockSpec((1,) + shape, lambda j: (j,) + (0,) * len(shape))


def shaped(shape, dtype=bf16):
    return jax.ShapeDtypeStruct(shape, dtype)


def by_piece(kernel, out_shape, in_specs, out_specs, scratch, args):
    return pl.pallas_call(
        kernel,
        out_shape=out_shape,
        grid=(4,),
        in_specs=in_specs,
        out_specs=out_specs,
        scratch_shapes=scratch,
        compiler_params=pltpu.CompilerParams(vmem_limit_bytes=48 * 2**20),
        cost_estimate=pl.CostEstimate(flops=0, bytes_accessed=0, transcendentals=0),
    )(*args)


def first_piece(action):
    pl.when(pl.program_id(0) == 0)(action)


def last_piece(action):
    pl.when(pl.program_id(0) == 3)(action)


def self_kernel(groups, x_ref, shift_ref, scale_ref, weight_ref, *refs):
    bias_ref = refs[0] if groups == 1 else None
    normed_ref, packed_ref, mixed_ref = refs[-3:]

    @first_piece
    def _():
        normed = norm_value(x_ref[...]) * (1.0 + scale_ref[...]) + shift_ref[...]
        normed_ref[...] = normed.astype(bf16)

    packed = product(normed_ref[...], weight_ref[0]).astype(bf16)
    packed_ref[0] = packed
    rows = 320 // groups
    for group in range(groups):
        mixed = []
        for head in range(2):
            queries, keys, values = (
                packed[group * rows : group * rows + rows, start : start + 72]
                for start in (72 * head, 144 + 72 * head, 288 + 72 * head)
            )
            bias = None if bias_ref is None else bias_ref[...]
            probability = softmax_value(queries, keys, bias).astype(bf16)
            mixed.append(product(probability, values))
        mixed_ref[0, group * rows : group * rows + rows, :] = jnp.concatenate(
            mixed, axis=1
        ).astype(bf16)


def self_forward(groups, hidden_state, shift, scale, weights, bias):
    specs = [whole((320, D)), whole((1, D)), whole((1, D)), part((D, 640))]
    args = [hidden_state, shift[None], scale[None], weights]
    if groups == 1:
        specs.append(whole((320, 320)))
        args.append(bias)
    return by_piece(
        partial(self_kernel, groups),
        [shaped((320, D)), shaped((4, 320, 640)), shaped((4, 320, 144))],
        specs,
        [whole((320, D)), part((320, 640)), part((320, 144))],
        [],
        args,
    )


def self_back_kernel(groups, extras, cuts, *refs):
    packed_ref, mixed_grad_ref, weight_ref, normed_ref = refs[:4]
    pairs = refs[4 : 4 + 2 * extras]
    bias_ref = refs[4 + 2 * extras] if groups == 1 else None
    normed_grad_ref, total_ref = refs[-2:]
    grad_refs = refs[-2 - len(cuts) : -2]
    packed, mixed_grad = packed_ref[0], mixed_grad_ref[0]
    rows = 320 // groups
    strips = []
    for group in range(groups):
        at = group * rows
        parts = []
        for head in range(2):
            queries, keys, values = (
                packed[at : at + rows, start : start + 72]
                for start in (72 * head, 144 + 72 * head, 288 + 72 * head)
            )
            bias = None if bias_ref is None else bias_ref[...]
            own_grad = mixed_grad[at : at + rows, 72 * head : 72 * head + 72]
            parts.append(head_back(queries, keys, values, own_grad, bias))
        line = [parts[head][which] for which in range(3) for head in range(2)]
        line.append(jnp.zeros((rows, 208), f32))
        strips.append(jnp.concatenate(line, axis=1).astype(bf16))
    packed_grad = strips[0] if groups == 1 else jnp.concatenate(strips, axis=0)
    width = weight_ref.shape[2]
    grad = outer_sum(normed_ref[...], packed_grad)
    if width > 640:
        grad = jnp.concatenate([grad, jnp.zeros((D, width - 640), f32)], axis=1)
    for n in range(extras):
        start = (384, 512, 640)[n]
        own = outer_sum(pairs[2 * n][...], pairs[2 * n + 1][0])
        lines = [grad[:, :start], grad[:, start : start + 256] + own, grad[:, start + 256 :]]
        grad = jnp.concatenate([line for line in lines if line.shape[1] > 0], axis=1)
    start = 0
    for cut, grad_ref in zip(cuts, grad_refs):
        grad_ref[0] = grad[:, start : start + cut].astype(bf16)
        start += cut
    back = product_back(packed_grad, weight_ref[0, :, :640])

    @first_piece
    def _():
        total_ref[...] = back

    @pl.when(pl.program_id(0) > 0)
    def _():
        total_ref[...] += back

    @last_piece
    def _():
        normed_grad_ref[...] = total_ref[...].astype(bf16)


def self_back(groups, packed, mixed_grad, weights, normed, pairs, bias, cuts):
    width = weights.shape[-1]
    specs = [part((320, 640)), part((320, 144)), part((D, width)), whole((320, D))]
    args = [packed, mixed_grad, weights, normed]
    for rows, window in pairs:
        specs += [whole((320, D)), part((320, 256))]
        args += [rows, window]
    if groups == 1:
        specs.append(whole((320, 320)))
        args.append(bias)
    results = by_piece(
        partial(self_back_kernel, groups, len(pairs), cuts),
        [shaped((4, D, cut)) for cut in cuts] + [shaped((320, D))],
        specs,
        [part((D, cut)) for cut in cuts] + [whole((320, D))],
        [pltpu.VMEM((320, D), f32)],
        args,
    )
    return results[:-1], results[-1]


def out_kernel(start, mixed_ref, weight_ref, out_ref):
    low = start // 128 * 128
    value = product(mixed_ref[...], weight_ref[0, :, low : low + 256])
    out_ref[0] = value[:, start - low : start - low + 144].astype(bf16)


def out_forward(mixed_rows, weights, start):
    return by_piece(
        partial(out_kernel, start),
        shaped((4, 320, 144)),
        [whole((320, D)), part(weights.shape[1:])],
        part((320, 144)),
        [],
        [mixed_rows, weights],
    )


def out_back_kernel(low, window_ref, weight_ref, out_ref, total_ref):
    back = product_back(window_ref[0], weight_ref[0, :, low : low + 256])

    @first_piece
    def _():
        total_ref[...] = back

    @pl.when(pl.program_id(0) > 0)
    def _():
        total_ref[...] += back

    @last_piece
    def _():
        for n in range(8):
            out_ref[n] = total_ref[:, 144 * n : 144 * n + 144].astype(bf16)


def out_back(window, weights, low):
    halves = by_piece(
        partial(out_back_kernel, low),
        shaped((8, 320, 144)),
        [part((320, 256)), part(weights.shape[1:])],
        whole((8, 320, 144)),
        [pltpu.VMEM((320, D), f32)],
        [window, weights],
    ).reshape(2, 4, 320, 144)
    core = lax.axis_index("c")
    keep = lax.dynamic_index_in_dim(halves, core, 0, keepdims=False)
    give = lax.dynamic_index_in_dim(halves, 1 - core, 0, keepdims=False)
    return (keep.astype(f32) + swap(give, "c").astype(f32)).astype(bf16)


def cross_kernel(x_ref, gain_ref, weight_ref, key_ref, value_ref, bias_ref, normed_ref, query_ref, mixed_ref):
    @first_piece
    def _():
        normed_ref[...] = (norm_value(x_ref[...]) * gain_ref[...]).astype(bf16)

    queries = product(normed_ref[...], weight_ref[0, :, 512:768]).astype(bf16)[:, 64:208]
    query_ref[0] = queries
    keys, values = key_ref[0], value_ref[0]
    mixed = []
    for head in range(2):
        own = slice(72 * head, 72 * head + 72)
        probability = softmax_value(queries[:, own], keys[:, own], bias_ref[...])
        mixed.append(product(probability.astype(bf16), values[:, own]))
    mixed_ref[0] = jnp.concatenate(mixed, axis=1).astype(bf16)


def cross_forward(hidden_state, gain, weights, keys, values, bias):
    return by_piece(
        cross_kernel,
        [shaped((320, D)), shaped((4, 320, 144)), shaped((4, 320, 144))],
        [whole((320, D)), whole((1, D)), part((D, 896))]
        + [part((128, 144)), part((128, 144)), whole((1, 128))],
        [whole((320, D)), part((320, 144)), part((320, 144))],
        [],
        [hidden_state, gain[None], weights, keys, values, bias],
    )


def cross_back_kernel(
    query_ref, key_ref, value_ref, grad_ref, weight_ref, bias_ref, window_ref, key_out, value_out, normed_ref, total_ref
):
    queries, keys, values, mixed_grad = query_ref[0], key_ref[0], value_ref[0], grad_ref[0]
    parts = []
    for head in range(2):
        own = slice(72 * head, 72 * head + 72)
        parts.append(
            head_back(queries[:, own], keys[:, own], values[:, own], mixed_grad[:, own], bias_ref[...])
        )
    zeros = jnp.zeros((320, 64), f32)
    window = jnp.concatenate(
        [zeros, parts[0][0], parts[1][0], zeros[:, :48]], axis=1
    ).astype(bf16)
    window_ref[0] = window
    key_out[0] = jnp.concatenate([parts[0][1], parts[1][1]], axis=1).astype(bf16)
    value_out[0] = jnp.concatenate([parts[0][2], parts[1][2]], axis=1).astype(bf16)
    back = product_back(window, weight_ref[0, :, 512:768])

    @first_piece
    def _():
        total_ref[...] = back

    @pl.when(pl.program_id(0) > 0)
    def _():
        total_ref[...] += back

    @last_piece
    def _():
        normed_ref[...] = total_ref[...].astype(bf16)


def cross_back(queries, keys, values, mixed_grad, weights, bias):
    return by_piece(
        cross_back_kernel,
        [shaped((4, 320, 256)), shaped((4, 128, 144)), shaped((4, 128, 144)), shaped((320, D))],
        [part((320, 144)), part((128, 144)), part((128, 144)), part((320, 144)), part((D, 896)), whole((1, 128))],
        [part((320, 256)), part((128, 144)), part((128, 144)), whole((320, D))],
        [pltpu.VMEM((320, D), f32)],
        [queries, keys, values, mixed_grad, weights, bias],
    )


GELU_SCALE = math.sqrt(2.0 / math.pi)


def down_halves(down_ref):
    blocks = [(y, 2 * z) for y in range(4) for z in range(2)]
    low = jnp.concatenate([down_ref[0, y, z] for y, z in blocks], axis=0)
    high = jnp.concatenate([down_ref[0, y, z + 1, :, :512] for y, z in blocks], axis=0)
    return low, high


def feed_kernel(x_ref, shift_ref, scale_ref, up_ref, down_ref, normed_ref, inner_ref, active_ref, out_ref, total_ref):
    @first_piece
    def _():
        normed = norm_value(x_ref[...]) * (1.0 + scale_ref[...]) + shift_ref[...]
        normed_ref[...] = normed.astype(bf16)

    inner = product(normed_ref[...], up_ref[0])
    inner_ref[0] = inner
    bent = jnp.tanh(GELU_SCALE * (inner + 0.044715 * inner * inner * inner))
    active = (0.5 * inner * (1.0 + bent)).astype(bf16)[:, :576]
    active_ref[0] = active
    low, high = down_halves(down_ref)

    @first_piece
    def _():
        total_ref[:, :640] = product(active, low)
        total_ref[:, 640:] = product(active, high)

    @pl.when(pl.program_id(0) > 0)
    def _():
        total_ref[:, :640] += product(active, low)
        total_ref[:, 640:] += product(active, high)

    @last_piece
    def _():
        out_ref[...] = total_ref[...].astype(bf16)


def feed_forward(hidden_state, shift, scale, up, down):
    return by_piece(
        feed_kernel,
        [shaped((320, D)), shaped((4, 320, 640), f32), shaped((4, 320, 576)), shaped((320, D))],
        [whole((320, D)), whole((1, D)), whole((1, D)), part((D, 640)), part((4, 4, 72, 640))],
        [whole((320, D)), part((320, 640)), part((320, 576)), whole((320, D))],
        [pltpu.VMEM((320, D), f32)],
        [hidden_state, shift[None], scale[None], up, down],
    )


def feed_back_kernel(
    grad_ref, inner_ref, active_ref, normed_ref, up_ref, down_ref, up_out, down_out, normed_grad_ref, total_ref
):
    low, high = down_halves(down_ref)
    low_grad, high_grad = grad_ref[:, :640], grad_ref[:, 640:]
    low_out = outer_sum(active_ref[0], low_grad).astype(bf16)
    high_out = outer_sum(active_ref[0], high_grad).astype(bf16)
    for block in range(8):
        rows = slice(72 * block, 72 * block + 72)
        down_out[0, block // 2, block % 2 * 2] = low_out[rows]
        down_out[0, block // 2, block % 2 * 2 + 1, :, :512] = high_out[rows]
        down_out[0, block // 2, block % 2 * 2 + 1, :, 512:] = jnp.zeros((72, 128), bf16)
    inner = inner_ref[0]
    active_grad = product_back(low_grad, low) + product_back(high_grad, high)
    active_grad = jnp.concatenate([active_grad, jnp.zeros((320, 64), f32)], axis=1)
    square = inner * inner
    bent = jnp.tanh(GELU_SCALE * inner * (1.0 + 0.044715 * square))
    slope = 0.5 * (1.0 + bent) + 0.5 * inner * (1.0 - bent * bent) * GELU_SCALE * (
        1.0 + 0.134145 * square
    )
    inner_grad = (active_grad * slope).astype(bf16)
    up_out[0] = outer_sum(normed_ref[...], inner_grad).astype(bf16)
    back = product_back(inner_grad, up_ref[0])

    @first_piece
    def _():
        total_ref[...] = back

    @pl.when(pl.program_id(0) > 0)
    def _():
        total_ref[...] += back

    @last_piece
    def _():
        normed_grad_ref[...] = total_ref[...].astype(bf16)


def feed_back(output_grad, inner, active, normed, up, down):
    return by_piece(
        feed_back_kernel,
        [shaped((4, D, 640)), shaped((4, 4, 4, 72, 640)), shaped((320, D))],
        [whole((320, D)), part((320, 640)), part((320, 576)), whole((320, D))]
        + [part((D, 640)), part((4, 4, 72, 640))],
        [part((D, 640)), part((4, 4, 72, 640)), whole((320, D))],
        [pltpu.VMEM((320, D), f32)],
        [output_grad, inner, active, normed, up, down],
    )


def words_kernel(text_ref, grad_ref, out_ref):
    out_ref[...] = outer_sum(text_ref[...], grad_ref[...]).astype(bf16)


def words_back(text, grad):
    return pl.pallas_call(
        words_kernel,
        out_shape=shaped((4096, 640)),
        grid=(8,),
        in_specs=[
            pl.BlockSpec((120, 512), lambda j: (0, j)),
            pl.BlockSpec((120, 640), lambda j: (0, 0)),
        ],
        out_specs=pl.BlockSpec((512, 640), lambda j: (j, 0)),
        compiler_params=pltpu.CompilerParams(vmem_limit_bytes=40 * 2**20),
        cost_estimate=pl.CostEstimate(flops=0, bytes_accessed=0, transcendentals=0),
    )(text, grad)


def both_cores(partial_rows):
    return partial_rows.astype(f32) + swap(partial_rows, "c").astype(f32)


def attention_block(groups, hidden_state, modulation, weights, bias):
    normed, packed, mixed = self_forward(
        groups, hidden_state, modulation[0], modulation[1], weights, bias
    )
    mixed_rows = apart(mixed)
    branch = apart(out_forward(mixed_rows, weights, 432)).astype(f32)
    stored = (hidden_state, normed, packed, mixed_rows, branch)
    return (hidden_state + modulation[2] * branch, stored)


def attention_block_back(groups, incoming, stored, modulation, weights, pairs, bias, earlier, cuts):
    hidden_state, normed, packed, mixed_rows, branch = stored
    gate_grad = jnp.sum(incoming * branch, axis=0)
    branch_grad = (modulation[2] * incoming).astype(bf16)
    window = windows(own_columns(branch_grad), 48)
    mixed_grad = after(out_back(window, weights, 384), earlier)
    weight_grad, normed_grad = self_back(
        groups, packed, mixed_grad, weights, normed, [(mixed_rows, window)] + pairs, bias, cuts
    )
    normed_grad = both_cores(normed_grad)
    normal_rows, inverse_std = normalize(hidden_state)
    scale_grad = jnp.sum(normed_grad * normal_rows, axis=0)
    shift_grad = jnp.sum(normed_grad, axis=0)
    upstream = incoming + norm_back(normal_rows, inverse_std, normed_grad * (1.0 + modulation[1]))
    return (upstream, weight_grad, (shift_grad, scale_grad, gate_grad))


def feed_block(hidden_state, modulation, up, down):
    normed, inner, active, output = feed_forward(
        hidden_state, modulation[3], modulation[4], up, down
    )
    output = both_cores(output)
    return (hidden_state + modulation[5] * output, (hidden_state, normed, inner, active, output))


def feed_block_back(incoming, stored, modulation, up, down):
    hidden_state, normed, inner, active, output = stored
    gate_grad = jnp.sum(incoming * output, axis=0)
    output_grad = (modulation[5] * incoming).astype(bf16)
    up_grad, down_grad, normed_grad = feed_back(output_grad, inner, active, normed, up, down)
    normed_grad = both_cores(normed_grad)
    normal_rows, inverse_std = normalize(hidden_state)
    scale_grad = jnp.sum(normed_grad * normal_rows, axis=0)
    shift_grad = jnp.sum(normed_grad, axis=0)
    upstream = incoming + norm_back(normal_rows, inverse_std, normed_grad * (1.0 + modulation[4]))
    return (upstream, up_grad, down_grad, (shift_grad, scale_grad, gate_grad))


def scatter_ring(grad):
    return lax.psum_scatter(grad, RING, scatter_dimension=0, tiled=False)


def own_columns(value):
    half = value.shape[1] // 2
    return jnp.where(lax.axis_index("c") == 0, value[:, :half], value[:, half:])


def local(
    latents,
    noise_sample,
    timesteps,
    text_states,
    text_lengths,
    cotangent,
    time_input,
    time_output,
    spatial_table,
    spatial_projection,
    spatial_output,
    spatial_up,
    spatial_down,
    temporal_table,
    temporal_projection,
    temporal_output,
    cross_query,
    cross_text,
    cross_output,
    cross_gain,
    temporal_up,
    temporal_down,
):
    core, far = lax.axis_index("c"), lax.axis_index("xh")
    clip = (lax.axis_index("y") * 4 + lax.axis_index("z")) * 2 + lax.axis_index("xl")
    me = clip * 4 + far * 2 + core

    sent = jnp.concatenate(
        [
            to_pieces(spatial_up, 1),
            to_pieces(spatial_projection, 3),
            to_pieces(spatial_output, 1),
            to_pieces(temporal_up, 1),
            to_pieces(temporal_projection, 3),
            to_pieces(temporal_output, 1),
            to_pieces(cross_query, 1),
            to_pieces(cross_output, 1),
        ],
        axis=2,
    )
    words = cross_text.reshape(4, 8, 2, 2, 2, 288).transpose(4, 3, 1, 0, 2, 5).reshape(4, 8, 2304)
    words = jnp.pad(words, ((0, 0), (0, 1), (0, 0)))
    near = lax.axis_index("xl")
    words = jnp.stack([jnp.where(near == 0, words, 0), jnp.where(near == 1, words, 0)])
    split_steps = jnp.stack([timesteps // 32, timesteps % 32], axis=1).reshape(-1).astype(bf16)
    note = [spatial_table.reshape(-1), temporal_table.reshape(-1), cross_gain, split_steps]
    note = jnp.pad(jnp.concatenate(note), (0, 9))[None]
    note = jnp.concatenate([time_input.reshape(9, 256), jnp.pad(note, ((0, 8), (0, 0)))], axis=1)
    note = jnp.broadcast_to(note, (8, 9, 384))
    sent = jnp.concatenate([sent, words.reshape(8, 9, 2304), note], axis=2)
    mine = swap_group(sent, GROUP)
    note = mine[..., 4896:].reshape(72, 384)
    words = lax.dynamic_slice_in_dim(mine[:, :8, 2592:4896], near * 4, 4, 0)
    words = words.reshape(4, 8, 4, 576).transpose(0, 2, 1, 3).reshape(128, 576)
    words = widen(words, 640)
    mine = mine[..., :2592].reshape(72, 2592)
    shards = jnp.stack([spatial_down, temporal_down])
    s_up = widen(mine[:, :576], 640)
    s_att = widen(mine[:, 576:1152], 640)
    t_up = widen(mine[:, 1152:1728], 640)
    t_att = widen(mine[:, 1728:2592], 896)
    downs = send_down(shards)

    near_words = by_core(words, swap(words, "xl"), "xl", 0)
    rings, first_done = fetch_rings(
        [
            (jnp.concatenate([t_up, s_att, downs[1], note], axis=1), "y"),
            (jnp.concatenate([s_up, t_att, downs[0]], axis=1), "z"),
        ],
        (),
    )
    t_up, att_down, note = place(rings[0], "y", 0, (640, 1280, 384))
    up_att, s_down = place(rings[1], "z", 0, (1536, 640))
    across = lax.all_gather(
        jnp.concatenate([att_down, s_down], axis=2), RING, axis=0, tiled=False
    )
    s_att, t_down, s_down = across[..., :640], across[..., 640:1280], across[..., 1280:]
    up_words = jnp.concatenate([t_up, near_words.reshape(4, 64, 640), widen(note, 640)], axis=1)
    rings, second_done = gather_rings([(up_att, "y"), (up_words, "z")], first_done)
    s_up, t_att = place(rings[0], "y", 0, (640, 896))
    (up_words,) = place(rings[1], "z", 1, (640,))
    t_up, words = up_words[:, :, :72], jnp.swapaxes(up_words[:, :, 72:136], 0, 1)
    notes = up_words[:, :, 136:, :384].reshape(16, 8, 9, 384)
    full_time_input = notes[..., :256].reshape(FREQ, D)
    notes = notes[:, :, 0, 256:].reshape(128, 128)
    steps = notes[::4, 117:119].astype(f32)
    steps = (steps[:, 0] * 32.0 + steps[:, 1]).astype(jnp.int32)
    embedded = time_features(steps, FREQ).astype(bf16)
    pre_time = product(embedded, full_time_input)
    lifted = jax.nn.silu(pre_time).astype(bf16)
    own_lifted = lax.dynamic_slice_in_dim(lifted, me * 9, 9, 1)
    shares = product(own_lifted, time_output)
    shares = swap_group(shares.reshape(128, 1728), ALL)
    s_up = lax.all_gather(s_up.reshape(D, 640), RING, axis=0, tiled=False)
    t_att = lax.all_gather(t_att.reshape(D, 896), RING, axis=0, tiled=False)
    words = lax.all_gather(words.reshape(1024, 640), "y", axis=0, tiled=False).reshape(4096, 640)
    t_up = lax.all_gather(t_up.reshape(D, 640), RING, axis=0, tiled=False)

    tables = notes[:, :108].reshape(128, 12, 9).transpose(1, 0, 2).reshape(2, 6, D)
    full_gain = notes[:, 108:117].reshape(D).astype(f32)
    shared = jnp.sum(shares, axis=0)
    shared = by_core(shared, swap(shared, "c"), "c", 0)
    shared = by_core(shared, swap(shared, "xh"), "xh", 0).reshape(6, D)
    rings, third_done = gather_rings([(s_att, "z"), (s_down, "y")], second_done)
    (s_att,) = place(rings[0], "z", 2, (640,))
    s_att = s_att.reshape(4, D, 640)
    (s_down,) = place(rings[1], "y", 1, (640,))
    rings, _ = gather_rings([(t_down, "z")], third_done)
    (t_down,) = place(rings[0], "z", 2, (640,))

    spatial_mod = tables[0].astype(f32) + shared
    temporal_mod = tables[1].astype(f32) + shared

    alpha_bars = noise_table(STEPS)
    picked = jnp.sum(jnp.where(jnp.arange(STEPS) == timesteps[0], alpha_bars, 0.0))
    signal_scale = jnp.sqrt(picked)

    frames = jnp.stack([latents[0, 0], noise_sample[0, 0]])
    other = swap(frames, "c")

    def noised(pair):
        return signal_scale * pair[0].astype(f32) + jnp.sqrt(1.0 - picked) * pair[1].astype(f32)

    hidden_state = by_core(noised(frames), noised(other), "c", 0)

    hidden_state, spatial_attention = attention_block(2, hidden_state, spatial_mod, s_att, None)
    hidden_state, spatial_mlp = feed_block(hidden_state, spatial_mod, s_up, s_down)

    def to_patches(rows):
        halves = rows.reshape(2, 2, 80, D)
        keep = lax.dynamic_index_in_dim(halves, far, 1, keepdims=False)
        give = lax.dynamic_index_in_dim(halves, 1 - far, 1, keepdims=False)
        return jnp.concatenate([keep, swap(give, "xh")], axis=0).reshape(320, D)

    patch_rows = to_patches(hidden_state.astype(bf16))
    own_cotangent = cotangent[0, 0]
    incoming = to_patches(by_core(own_cotangent, swap(own_cotangent, "c"), "c", 0)).astype(f32)

    row = jnp.arange(320) % 80
    patch_bias = jnp.where(row[:, None] == row[None], 0.0, MASK_FILL)

    hidden_state = patch_rows.astype(f32)
    hidden_state, temporal_attention = attention_block(
        1, hidden_state, temporal_mod, t_att, patch_bias
    )
    text_order = text_states[0]
    text_rows = product(text_order, tie(words, temporal_attention[3]))[:, :576].astype(bf16)
    other_text = swap(text_rows, "xh")
    def text_pieces(value):
        pieces = jnp.swapaxes(value.reshape(120, 4, 144), 0, 1)
        return jnp.pad(pieces, ((0, 0), (0, 8), (0, 0)))

    text_keys = text_pieces(by_core(text_rows[:, :288], other_text[:, :288], "xh", 1))
    text_values = text_pieces(by_core(text_rows[:, 288:], other_text[:, 288:], "xh", 1))
    text_bias = jnp.where(jnp.arange(128) < text_lengths[0], 0.0, MASK_FILL)[None]
    cross_state = hidden_state
    cross_normed, cross_queries, cross_mixed = cross_forward(
        cross_state, full_gain, t_att, text_keys, text_values, text_bias
    )
    cross_mixed = apart(cross_mixed)
    hidden_state = cross_state + apart(out_forward(cross_mixed, t_att, 720)).astype(f32)
    hidden_state, temporal_mlp = feed_block(hidden_state, temporal_mod, t_up, t_down)

    finished = hidden_state.astype(bf16).reshape(4, 80, D)
    keep = lax.dynamic_index_in_dim(finished, core, 0, keepdims=False)
    give = lax.dynamic_index_in_dim(finished, 2 + core, 0, keepdims=False)
    activations = by_core(keep, swap(give, "xh"), "xh", 0)[None, None]

    incoming, t_up_grad, t_down_grad, t_mlp_mod = feed_block_back(
        incoming, temporal_mlp, temporal_mod, t_up, t_down
    )
    t_up_grad = scatter_ring(t_up_grad)
    t_down_grad = scatter_ring(t_down_grad.reshape(4, D, 640))
    cross_grad = incoming.astype(bf16)
    out_window = windows(own_columns(cross_grad), 80)
    cross_mixed_grad = out_back(out_window, t_att, 640)
    query_window, key_grad, value_grad, normed_grad = cross_back(
        cross_queries, text_keys, text_values, cross_mixed_grad, t_att, text_bias
    )
    normed_grad = both_cores(normed_grad)
    normal_rows, inverse_std = normalize(cross_state)
    gain_grad = jnp.sum(normed_grad * normal_rows, axis=0)
    incoming = incoming + norm_back(normal_rows, inverse_std, normed_grad * full_gain)
    key_grad = jnp.swapaxes(key_grad[:, :120], 0, 1).reshape(120, 576)
    value_grad = jnp.swapaxes(value_grad[:, :120], 0, 1).reshape(120, 576)

    def text_half(which):
        def half(value):
            return lax.dynamic_slice_in_dim(value, which * 288, 288, 1)

        return jnp.concatenate([half(key_grad), half(value_grad)], axis=1)

    text_grad = text_half(far).astype(f32) + swap(text_half(1 - far), "xh").astype(f32)
    words_grad = words_back(text_order, widen(text_grad.astype(bf16), 640))
    incoming, t_att_grad, t_att_mod = attention_block_back(
        1,
        incoming,
        temporal_attention,
        temporal_mod,
        t_att,
        [(cross_normed, query_window), (cross_mixed, out_window)],
        patch_bias,
        (text_grad, t_up_grad),
        (896,),
    )
    t_mod_grad = jnp.stack(t_att_mod + t_mlp_mod)

    back = incoming.astype(bf16).reshape(4, 80, D)
    theirs = swap(back[2:], "xh")
    t_att_grad = scatter_ring(tie(t_att_grad[0], t_down_grad))


    frame_grad = by_core(back[:2], theirs, "xh", 1).reshape(320, D).astype(f32)
    words_grad = tie(words_grad, t_att_grad).reshape(4, 1024, 640)
    words_grad = lax.psum_scatter(words_grad, "y", scatter_dimension=0, tiled=False)
    words_grad = words_grad.reshape(4, 256, 640)
    words_grad = lax.psum_scatter(words_grad, "z", scatter_dimension=0, tiled=False)
    words_grad = words_grad.reshape(2, 128, 640)
    words_grad = lax.dynamic_index_in_dim(words_grad, near, 0, keepdims=False).astype(f32) + swap(
        lax.dynamic_index_in_dim(words_grad, 1 - near, 0, keepdims=False), "xl"
    ).astype(f32)
    words_grad = words_grad.astype(bf16)
    frame_grad, s_up_grad, s_down_grad, s_mlp_mod = feed_block_back(
        frame_grad, spatial_mlp, spatial_mod, s_up, s_down
    )
    s_up_grad = s_up_grad.reshape(4, 4, 4, 72, 640)
    (s_up_grad, s_down_grad), s_done, _ = scatter_rings(
        [([(s_up_grad, 2)], "z"), ([(s_down_grad, 1)], "y")], ()
    )
    frame_grad, s_att_grad, s_att_mod = attention_block_back(
        2, frame_grad, spatial_attention, spatial_mod, s_att, [], None, (s_done, t_down_grad), (384, 256)
    )
    t_up_grad = tie(t_up_grad, s_att_grad[0])
    t_grads = jnp.concatenate([t_up_grad, t_att_grad, t_down_grad], axis=1)
    t_grads = t_grads.reshape(4, 288, 2176)
    t_grads = lax.psum_scatter(t_grads, "y", scatter_dimension=0, tiled=False)
    t_grads = t_grads.reshape(4, 72, 2176)
    t_grads = lax.psum_scatter(t_grads, "z", scatter_dimension=0, tiled=False)
    latent_grad = signal_scale * lax.dynamic_index_in_dim(frame_grad.reshape(2, 160, D), core, 0)
    s_mod_grad = jnp.stack(s_att_mod + s_mlp_mod)
    s_att_grad = [grad.reshape(4, 4, 4, 72, -1) for grad in s_att_grad]
    (att_x_y, att_x_z), _, done = scatter_rings(
        [([(s_att_grad[0], 2)], "z"), ([(s_att_grad[1], 1)], "y")], ()
    )
    (up, down), done = sum_rings(
        [([(s_up_grad, 1), (att_x_y, 1)], "y"), ([(s_down_grad, 0), (att_x_z, 0)], "x")], done
    )
    (up, down), done = sum_rings([([(up, 0)], "x"), ([(down, 0)], "z")], done)
    downs = return_down(jnp.stack([down[:, :640], t_grads[:, 1536:]])).astype(f32)
    s_down_done, t_down_done = downs[0], downs[1]
    words_grad = swap_group(words_grad[:, :576].reshape(4, 32, 576), SEQ)
    words_grad = words_grad.reshape(2, 2, 32, 2, 288).transpose(2, 3, 1, 0, 4).reshape(32, 2304)

    returned = jnp.concatenate(
        [
            up[:, :576],
            up[:, 640:],
            down[:, 640:832],
            t_grads[:, :576],
            t_grads[:, 640:1504],
        ],
        axis=1,
    )
    returned = swap_group(returned.reshape(8, 9, 2592), GROUP).astype(f32)
    s_up_grad = from_pieces(returned[..., :576], 1)
    s_proj_grad = from_pieces(returned[..., 576:1008], 3)
    s_out_grad = from_pieces(returned[..., 1008:1152], 1)
    t_up_grad = from_pieces(returned[..., 1152:1728], 1)
    t_proj_grad = from_pieces(returned[..., 1728:2160], 3)
    t_out_grad = from_pieces(returned[..., 2160:2304], 1)
    x_query_grad = from_pieces(returned[..., 2304:2448], 1)
    x_out_grad = from_pieces(returned[..., 2448:], 1)

    shared_grad = (s_mod_grad + t_mod_grad).reshape(4, 1728)
    shared_grad = shared_grad + swap(shared_grad, "xh")
    quarter = lax.dynamic_index_in_dim(shared_grad, far * 2 + core, 0, keepdims=False)
    table_part = jnp.stack([s_mod_grad, t_mod_grad]).reshape(12, 128, 9).transpose(1, 0, 2)
    table_part = jnp.concatenate([table_part.reshape(128, 108), gain_grad.reshape(128, 9)], axis=1)
    table_part = jnp.where(core == 0, table_part, 0.0)
    letter = jnp.concatenate(
        [jnp.broadcast_to(quarter, (128, 1728)), table_part, jnp.zeros((128, 75), f32)], axis=1
    )
    letters = swap_group(letter, ALL)
    all_shared = letters[:, :1728].reshape(32, 6 * D)
    table_sum = jnp.sum(letters[:, 1728:1845], axis=0)
    s_table_grad = table_sum[:54].reshape(6, 9)
    t_table_grad = table_sum[54:108].reshape(6, 9)
    cross_gain_grad = table_sum[108:]

    def exact(a, b, dims):
        return lax.dot_general(
            a, b, (dims, ((), ())), precision=lax.Precision.HIGHEST, preferred_element_type=f32
        )

    time_output_grad = exact(own_lifted.astype(f32), all_shared, ((0,), (0,)))
    lifted_grad = exact(all_shared, time_output.astype(f32), ((1,), (1,)))
    own_pre = lax.dynamic_slice_in_dim(pre_time, me * 9, 9, 1)
    own_pre_grad = jax.vjp(jax.nn.silu, own_pre)[1](lifted_grad)[0]
    card = jnp.broadcast_to(widen(own_pre_grad.reshape(288), 384), (128, 384))
    cards = swap_group(card, ALL)[:, :288].reshape(128, 32, 9)
    pre_grad = cards.transpose(1, 0, 2).reshape(32, D)
    own_embedded = lax.dynamic_slice_in_dim(embedded, me * 2, 2, 1).astype(f32)
    time_input_grad = exact(own_embedded, pre_grad, ((0,), (0,)))

    return (
        activations,
        latent_grad[None],
        time_input_grad,
        time_output_grad,
        s_table_grad,
        s_proj_grad,
        s_out_grad,
        s_up_grad,
        s_down_done,
        t_table_grad,
        t_proj_grad,
        t_out_grad,
        x_query_grad,
        words_grad.astype(f32),
        x_out_grad,
        cross_gain_grad,
        t_up_grad,
        t_down_done,
    )


def solution(mesh):
    fine = Mesh(mesh.devices.reshape(4, 4, 2, 2, 2), ALL)
    frames = P(CLIP, SEQ, None, None)
    rows = P(ALL, None)
    columns = P(None, ALL)
    in_specs = (
        frames,
        frames,
        P(CLIP),
        P(CLIP, None, None),
        P(CLIP),
        frames,
        rows,
        rows,
        columns,
        rows,
        rows,
        rows,
        rows,
        columns,
        rows,
        rows,
        rows,
        rows,
        rows,
        P(ALL),
        rows,
        rows,
    )
    out_specs = (
        frames,
        frames,
        rows,
        rows,
        columns,
        rows,
        rows,
        rows,
        rows,
        columns,
        rows,
        rows,
        rows,
        rows,
        rows,
        P(ALL),
        rows,
        rows,
    )
    return jax.shard_map(local, mesh=fine, in_specs=in_specs, out_specs=out_specs, check_vma=False)
```
